32 devices in a mesh: row: 4 (over x, core), col: 8 (over z, y).
Axes of the slice: x: 2, y: 2, z: 4, core: 2. Of those that a mesh axis runs over, the one named last changes fastest.
Arguments:
- activations: bfloat16 [1024, 8192], P('col', 'row'), may hold values from -6 to 6
- out_grads: bfloat16 [1024, 22016], P('row', 'col'), may hold values from -48 to 48
- basis: float32 [8192, 512], P('row'), may hold values from -0.0625 to 0.0625
- row_moment: float32 [512], P('row'), may hold values from 10240 to 102400
- col_moment: float32 [22016], P('col'), may hold values from 1024 to 204800
Outputs:
- weight_update: float32 [8192, 22016], P('row', 'col')
- row_next: float32 [512], P('row')
- col_next: float32 [22016], P('col')
The draws below stay inside these ranges and needn't reach their ends.
All inputs are finite; a program needn't handle non-finite values.
Results may differ from the reference program's by a relative error of at most 0.0003.
Values may be sent and summed in bfloat16 or wider, within the bound.
No kernel may reach another device: no remote copies, remote signals or barrier semaphores. Data moves between devices by JAX's collectives and lax.ppermute only.
A program may use at most 128 MiB of HBM per device.

```python
import math
import jax
import jax.numpy as jnp
from jax import lax

D = 8192
F = 22016
R = 512
TOKENS = 1024
N_COL = 8


def draw_out_grads(key, part):
    key = jax.random.fold_in(key, 7)
    noise_key, rough_key, token_key = jax.random.split(key, 3)
    columns = jnp.arange(F).astype(jnp.float32) / F
    ramp = jnp.exp(jnp.log(10.0) * columns)
    rough = jnp.exp(jax.random.uniform(rough_key, (F,), jnp.float32, jnp.log(0.5), jnp.log(2.0)))
    token_scale = jnp.exp(jax.random.uniform(token_key, (TOKENS, 1), jnp.float32, jnp.log(0.5), jnp.log(2.0)))
    base = jnp.clip(jax.random.normal(noise_key, (TOKENS, F), jnp.float32), -6.0, 6.0)
    values = base * token_scale * ramp[None, :] * rough[None, :]
    return jnp.clip(values, -48.0, 48.0).astype(jnp.bfloat16)


def levels(stream_key, dims, cuts, least, largest):
    def one(axis_at, shards_of):
        draws = jax.random.uniform(jax.random.fold_in(jax.random.fold_in(stream_key, 6), axis_at), (shards_of,), jnp.float32, least / len(cuts), largest / len(cuts))
        return jnp.repeat(jnp.exp(draws), dims[axis_at] // shards_of).reshape((-1,) + (1,) * (len(dims) - axis_at - 1))

    factor_of = one(*cuts[0])
    for cut in cuts[1:]:
        factor_of = factor_of * one(*cut)
    return factor_of


def bell_draw(key, shape, scale, most, pieces=(), kind=jnp.bfloat16):
    values = jax.random.normal(key, shape, jnp.float32) * scale
    if len(pieces) > 0:
        values = levels(key, shape, pieces, -0.22, 0.18) * values
    return jnp.clip(values, min=-most, max=most).astype(kind)


def setup_inputs(seed: int = 0) -> dict:
    key_of = jax.random.split(jax.random.key(seed), 6)
    activations = bell_draw(key_of[0], (TOKENS, D), 1.0, 6.0, ((0, 8), (1, 4)))
    out_grads = draw_out_grads(jax.random.fold_in(key_of[5], 71), 0)
    basis = bell_draw(key_of[2], (D, R), D ** -0.5, 0.0625, ((0, 4),), jnp.float32)
    row_moment = jnp.clip(jnp.exp(math.log(102400.0) - 2.3025851 * jax.random.uniform(key_of[3], (R,), jnp.float32) ** levels(key_of[3], (R,), ((0, 4),), -0.2, 0.2)), 10240.0, 102400.0)
    col_moment = jnp.clip(jnp.exp(math.log(204800.0) - 5.2983174 * jax.random.uniform(key_of[4], (F,), jnp.float32) ** levels(key_of[4], (F,), ((0, 8),), -0.2, 0.2)), 1024.0, 204800.0)
    return dict(activations=activations, out_grads=out_grads, basis=basis, row_moment=row_moment, col_moment=col_moment)


beta_two = 0.8
scale_alpha = 0.25
epsilon = 1e-30

def reference(activations, out_grads, basis, row_moment, col_moment):
    width = F // N_COL
    blocks = out_grads.reshape(TOKENS, N_COL, width).transpose(1, 0, 2)

    def project(block):
        gradient = lax.dot_general(activations, block, (((0,), (0,)), ((), ())), preferred_element_type=jnp.float32)
        return lax.dot_general(basis, gradient, (((0,), (0,)), ((), ())), precision=lax.Precision.HIGHEST)
    projected = lax.map(project, blocks).transpose(1, 0, 2).reshape(R, F)
    squares = projected * projected + epsilon
    row_next = beta_two * row_moment + (1.0 - beta_two) * lax.optimization_barrier(jnp.mean(squares, axis=1))
    col_next = beta_two * col_moment + (1.0 - beta_two) * lax.optimization_barrier(jnp.mean(squares, axis=0))
    second = row_next[:, None] * col_next[None, :] / jnp.mean(row_next)
    normalized = projected / jnp.sqrt(second)
    weight_update = scale_alpha * jnp.dot(basis, normalized, precision=lax.Precision.HIGHEST)
    return (weight_update, row_next, col_next)
```

```python
import functools

import jax
import jax.numpy as jnp
import numpy as np
from jax import lax
from jax.experimental import pallas as pl
from jax.experimental.pallas import tpu as pltpu
from jax.sharding import PartitionSpec as P

beta_two = 0.8
scale_alpha = 0.25
epsilon = 1e-30
CORES = 2
CHUNKS = 2
TILES = 2
f32 = jnp.float32
bf16 = jnp.bfloat16
f8 = jnp.float8_e4m3fn
MIB = 1 << 20
CODE_TOP = 181.0
TOP_ROWS = 16
VMEM = pl.BlockSpec(memory_space=pltpu.VMEM)
SMEM = pl.BlockSpec(memory_space=pltpu.SMEM)


def split(value):
    high = value.astype(bf16)
    return high, (value - high.astype(f32)).astype(bf16)


def tile_of(size, most, unit):
    return max(t for t in range(unit, most + 1, unit) if size % t == 0)


def low_kernel(streams, where_ref, act_ref, *refs):
    basis = refs[:streams]
    mine_ref, other_ref, acc_ref = refs[streams:]
    step = pl.program_id(0)

    @pl.when(step == 0)
    def _():
        acc_ref[...] = jnp.zeros_like(acc_ref)

    tile = basis[0].shape[0]
    total = acc_ref[...]
    for n, ref in enumerate(basis):
        high, low = split(ref[...])
        acts = act_ref[:, n * tile : (n + 1) * tile]
        total = total + jnp.dot(acts, high, preferred_element_type=f32)
        total = total + jnp.dot(acts, low, preferred_element_type=f32)
    acc_ref[...] = total

    @pl.when(step == pl.num_programs(0) - 1)
    def _():
        half = mine_ref.shape[1]
        core = where_ref[0]
        mine_ref[...] = acc_ref[:, pl.ds(pl.multiple_of(core * half, half), half)]
        other_ref[...] = acc_ref[:, pl.ds(pl.multiple_of((1 - core) * half, half), half)]


def low_partial(where, acts, basis):
    tokens, depth = acts.shape
    rank = basis.shape[1]
    steps, streams = 2, 4
    tile = depth // (steps * streams)
    half = jax.ShapeDtypeStruct((tokens, rank // 2), f32)

    def stream(n):
        return pl.BlockSpec((tile, rank), lambda i, s: (i * streams + n, 0))

    return pl.pallas_call(
        functools.partial(low_kernel, streams),
        out_shape=(half, half),
        grid_spec=pltpu.PrefetchScalarGridSpec(
            num_scalar_prefetch=1,
            grid=(steps,),
            in_specs=[pl.BlockSpec((tokens, tile * streams), lambda i, s: (0, i))]
            + [stream(n) for n in range(streams)],
            out_specs=[pl.BlockSpec((tokens, rank // 2), lambda i, s: (0, 0))] * 2,
            scratch_shapes=[pltpu.VMEM((tokens, rank), f32)],
        ),
        compiler_params=pltpu.CompilerParams(vmem_limit_bytes=56 * MIB),
        cost_estimate=pl.CostEstimate(
            flops=4 * tokens * depth * rank, bytes_accessed=6 * depth * rank, transcendentals=0
        ),
        name="low_partial",
    )(where, acts, *[basis] * streams)


def turn_kernel(basis_ref, high_ref, small_ref):
    rank = basis_ref.shape[1]
    turned = basis_ref[...].T
    high = turned.astype(bf16)
    high_ref[...] = high
    small_ref[:rank, :] = ((turned - high.astype(f32)) * 2.0**20).astype(f8)
    small_ref[rank:, :] = (turned * 2.0**12).astype(f8)


def turn_basis(basis):
    rows, rank = basis.shape
    tile = tile_of(rows, 256, 128)
    return pl.pallas_call(
        turn_kernel,
        out_shape=[
            jax.ShapeDtypeStruct((rank, rows), bf16),
            jax.ShapeDtypeStruct((2 * rank, rows), f8),
        ],
        grid=(rows // tile,),
        in_specs=[pl.BlockSpec((tile, rank), lambda i: (i, 0))],
        out_specs=[
            pl.BlockSpec((rank, tile), lambda i: (0, i)),
            pl.BlockSpec((2 * rank, tile), lambda i: (0, i)),
        ],
        compiler_params=pltpu.CompilerParams(vmem_limit_bytes=8 * MIB),
        cost_estimate=pl.CostEstimate(flops=0, bytes_accessed=8 * rows * rank, transcendentals=0),
        name="turn_basis",
    )(basis)


def encode_kernel(*refs):
    out_ref = refs[-1]
    tokens, lanes = refs[0].shape
    value = refs[0][...]
    for ref in refs[1:-1]:
        value = value + ref[...]
    size = jnp.abs(value)
    top = (jnp.max(size, axis=0, keepdims=True) * (1.0 + 2.0**-7)).astype(bf16).astype(f32)
    top = jnp.maximum(top, 1e-36)
    code = size * (CODE_TOP / top)
    for _ in range(4):
        code = code * code
    out_ref[:tokens, :] = jnp.where(value < 0, -code, code).astype(bf16)
    out_ref[tokens:, :] = jnp.broadcast_to(top, (TOP_ROWS, lanes)).astype(bf16)


def encode(*blocks):
    tokens, lanes = blocks[0].shape
    return pl.pallas_call(
        encode_kernel,
        out_shape=jax.ShapeDtypeStruct((tokens + TOP_ROWS, lanes), bf16),
        in_specs=[VMEM] * len(blocks),
        out_specs=VMEM,
        compiler_params=pltpu.CompilerParams(vmem_limit_bytes=4 * MIB),
        cost_estimate=pl.CostEstimate(
            flops=0, bytes_accessed=8 * tokens * lanes, transcendentals=0
        ),
        name="encode",
    )(*blocks)


def decode(ref):
    tokens = ref.shape[0] - TOP_ROWS
    code = ref[:tokens, :].astype(f32)
    size = jnp.abs(code)
    for _ in range(4):
        size = lax.rsqrt(size)
    size = size * (ref[tokens : tokens + 1, :].astype(f32) * (1.0 / CODE_TOP))
    return jnp.where(code < 0, -size, size)


def assemble_kernel(blocks, offset, where_ref, *refs):
    mine, other = refs[:blocks], refs[blocks : 2 * blocks]
    high_ref, low_ref = refs[2 * blocks :]
    half = high_ref.shape[1] // 2
    core = where_ref[0]
    for refs_of, at in ((mine, core), (other, 1 - core)):
        lanes = pl.ds(pl.multiple_of(at * half, half), half)
        for b in range(blocks):
            tokens = refs_of[b].shape[0] - TOP_ROWS
            rows = pl.ds(pl.multiple_of(where_ref[offset + b] * tokens, tokens), tokens)
            high, low = split(decode(refs_of[b]))
            high_ref[rows, lanes] = high
            low_ref[rows, lanes] = low


def assemble(where, mine, other, offset):
    blocks = len(mine)
    tokens, half = mine[0].shape
    shape = (blocks * (tokens - TOP_ROWS), 2 * half)
    return pl.pallas_call(
        functools.partial(assemble_kernel, blocks, offset),
        out_shape=[jax.ShapeDtypeStruct(shape, bf16)] * 2,
        in_specs=[SMEM] + [VMEM] * (2 * blocks),
        out_specs=[VMEM] * 2,
        compiler_params=pltpu.CompilerParams(vmem_limit_bytes=4 * MIB),
        cost_estimate=pl.CostEstimate(
            flops=0, bytes_accessed=8 * shape[0] * shape[1], transcendentals=0
        ),
        name="assemble",
    )(where, *mine, *other)


def cut_kernel(starts_at, counts, where_ref, grads_ref, *refs):
    outs, sem = refs[:-1], refs[-1]
    copies = []
    for n, out in enumerate(outs):
        rows = out.shape[0]
        at = pl.ds(pl.multiple_of(where_ref[starts_at + n] * 16, 16), rows)
        copies.append(pltpu.make_async_copy(grads_ref.at[at, :], out, sem.at[n]))
    for copy in copies:
        copy.start()
    for copy in copies:
        copy.wait()


def cut(where, grads, sizes, starts_at):
    return pl.pallas_call(
        functools.partial(cut_kernel, starts_at, len(sizes)),
        out_shape=[jax.ShapeDtypeStruct((size, grads.shape[1]), bf16) for size in sizes],
        in_specs=[SMEM, pl.BlockSpec(memory_space=pl.ANY)],
        out_specs=[VMEM] * len(sizes),
        scratch_shapes=[pltpu.SemaphoreType.DMA((len(sizes),))],
        compiler_params=pltpu.CompilerParams(vmem_limit_bytes=4 * MIB),
        cost_estimate=pl.CostEstimate(
            flops=0, bytes_accessed=4 * sum(sizes) * grads.shape[1], transcendentals=0
        ),
        name="cut",
    )(where, grads)


def project_kernel(
    pieces, step, start_at, rows_at, first, where_ref, high_ref, low_ref, moment_ref, most_ref, *refs
):
    out_ref, colnext_ref, sums_ref, top_ref = refs[len(refs) - 4 :]
    grads, moments = refs[:pieces], refs[pieces : len(refs) - 4]
    rows, rank = out_ref.shape
    tokens = grads[0].shape[1]
    order = [
        pl.ds(pl.multiple_of(where_ref[rows_at + p] * tokens, tokens), tokens)
        for p in range(pieces)
    ]
    high = jnp.concatenate([high_ref[at, :] for at in order], axis=0)
    low = jnp.concatenate([low_ref[at, :] for at in order], axis=0)
    sums = jnp.zeros((1, rank), f32)
    if first:
        lanes = moments[0].shape[1]
        owner = lax.broadcasted_iota(jnp.int32, (1, rank), 1) // lanes
        for n, ref in enumerate(moments):
            wide = jnp.concatenate([ref[...]] * (rank // lanes), axis=1)
            sums = jnp.where(owner == where_ref[rows_at + n], wide, sums)
        sums = sums * jnp.where(where_ref[1] == 1, first, 0.0)
    top = most_ref[...]
    for begin in range(0, rows, step):
        at = pl.ds(pl.multiple_of(where_ref[start_at] * 16 + begin, 16), step)
        here = slice(begin, begin + step)
        grad = jnp.concatenate(
            [g[at, :] for g in grads[:2]] + [g[here, :] for g in grads[2:]], axis=1
        )
        total = jnp.dot(grad, high, preferred_element_type=f32) + jnp.dot(
            grad, low, preferred_element_type=f32
        )
        squares = total * total
        sums = sums + jnp.sum(squares, axis=0, keepdims=True)
        quarter = sum(squares[:, n : n + 128] for n in range(0, rank, 128))
        col_next = beta_two * moment_ref[at, :] + (1.0 - beta_two) * (
            jnp.sum(quarter, axis=1, keepdims=True) / rank + epsilon
        )
        part = total * lax.rsqrt(col_next)
        top = jnp.maximum(top, jnp.max(jnp.abs(part), axis=0, keepdims=True))
        out_ref[here, :] = part
        long = colnext_ref.shape[1]
        wide = jnp.broadcast_to(col_next, (step, 128))
        if long > step:
            wide = jnp.concatenate([wide, jnp.zeros((long - step, 128), f32)], axis=0)
        colnext_ref[begin // step : begin // step + 1, :] = wide.T[:1, :]
    sums_ref[...] = sums
    top_ref[...] = top


def project(where, high, low, moment, most, grads, moments, rows, step, start_at, rows_at, first):
    tokens, rank = high.shape
    long = -(-step // 128) * 128
    return pl.pallas_call(
        functools.partial(project_kernel, len(grads), step, start_at, rows_at, first),
        out_shape=[
            jax.ShapeDtypeStruct((rows, rank), f32),
            jax.ShapeDtypeStruct((rows // step, long), f32),
            jax.ShapeDtypeStruct((1, rank), f32),
            jax.ShapeDtypeStruct((1, rank), f32),
        ],
        in_specs=[SMEM] + [VMEM] * (4 + len(grads) + len(moments)),
        out_specs=[VMEM] * 4,
        compiler_params=pltpu.CompilerParams(vmem_limit_bytes=16 * MIB),
        cost_estimate=pl.CostEstimate(
            flops=4 * tokens * rows * rank,
            bytes_accessed=2 * rows * tokens + 4 * tokens * rank + 4 * rows * rank,
            transcendentals=0,
        ),
        name="project",
    )(where, high, low, moment, most, *grads, *moments)


def update_kernel(
    count, parts, rows_at, order_at, where_ref, sums_ref, most_ref, high_ref, small_ref, *refs
):
    part_refs, col_refs = refs[:parts], refs[parts : 2 * parts]
    out_ref, rownext_ref, colnext_ref, lhs_ref, lhs_small_ref, scale_ref = refs[2 * parts :]
    tile, rank = lhs_ref.shape
    step = pl.program_id(0)

    @pl.when(step == 0)
    def _():
        row_next = (1.0 - beta_two) * (sums_ref[...] / count + epsilon)
        rows = rownext_ref.shape[1]
        held = jnp.zeros((1, rows), f32)
        for r in range(rank // rows):
            held = jnp.where(where_ref[rows_at] == r, row_next[:, r * rows : (r + 1) * rows], held)
        rownext_ref[...] = held
        scale = scale_alpha * lax.rsqrt(row_next) * jnp.sqrt(
            jnp.mean(row_next, axis=1, keepdims=True)
        )
        strip = colnext_ref.shape[1]
        number = 0
        for ref in col_refs:
            for n in range(ref.shape[0]):
                at = pl.ds(where_ref[order_at + number * TILES] // TILES, 1)
                colnext_ref[at, :] = ref[n : n + 1, :strip]
                number += 1
        top = jnp.maximum(jnp.max(scale * most_ref[...], axis=1, keepdims=True), 1e-30)
        scale_ref[0:1, :] = scale
        scale_ref[1:2, :] = jnp.broadcast_to(2.0**7 / top, (1, rank))
        scale_ref[2:3, :] = jnp.broadcast_to(top * 2.0**-27, (1, rank))

    first = 0
    for part_ref in part_refs:
        tiles = part_ref.shape[0] // tile

        @pl.when((step >= first) & (step < first + tiles))
        def _():
            at = pl.ds(pl.multiple_of((step - first) * tile, 8), tile)
            value = part_ref[at, :] * scale_ref[0:1, :]
            high = value.astype(bf16)
            grow = scale_ref[1:2, :]
            lhs_ref[...] = high
            lhs_small_ref[:, :rank] = (value * grow).astype(f8)
            lhs_small_ref[:, rank:] = ((value - high.astype(f32)) * (grow * 2.0**8)).astype(f8)

        first += tiles

    out_ref[...] = jnp.dot(
        lhs_ref[...], high_ref[...], preferred_element_type=f32
    ) + scale_ref[2:3, 0:1] * jnp.dot(
        lhs_small_ref[...], small_ref[...], preferred_element_type=f32
    )


def update(where, sums, most, high, small, parts, cols, strip, hidden, n_row, rows_at, order_at):
    rank, rows = high.shape
    columns = sum(part.shape[0] for part in parts)
    tile = strip // TILES
    steps = columns // tile
    return pl.pallas_call(
        functools.partial(update_kernel, float(hidden), len(parts), rows_at, order_at),
        out_shape=[
            jax.ShapeDtypeStruct((columns, rows), f32),
            jax.ShapeDtypeStruct((1, rank // n_row), f32),
            jax.ShapeDtypeStruct((columns // strip, strip), f32),
        ],
        grid_spec=pltpu.PrefetchScalarGridSpec(
            num_scalar_prefetch=1,
            grid=(steps,),
            in_specs=[VMEM] * (4 + 2 * len(parts)),
            out_specs=[
                pl.BlockSpec((tile, rows), lambda i, s: (s[order_at + i], 0)),
                pl.BlockSpec((1, rank // n_row), lambda i, s: (0, 0)),
                pl.BlockSpec((columns // strip, strip), lambda i, s: (0, 0)),
            ],
            scratch_shapes=[
                pltpu.VMEM((tile, rank), bf16),
                pltpu.VMEM((tile, 2 * rank), f8),
                pltpu.VMEM((8, rank), f32),
            ],
        ),
        compiler_params=pltpu.CompilerParams(vmem_limit_bytes=20 * MIB),
        cost_estimate=pl.CostEstimate(
            flops=4 * columns * rank * rows, bytes_accessed=4 * columns * rows, transcendentals=0
        ),
        name="update",
    )(where, sums, most, high, small, *parts, *cols)


def per_device(n_row, n_col, activations, out_grads, basis, row_moment, col_moment):
    chips = n_row // CORES
    columns = col_moment.shape[0]
    hidden = columns * n_col
    rank = basis.shape[1]
    width = -(-columns // (32 * chips)) * 32
    pad = width * chips - columns
    rows = width // CHUNKS
    ring = [0, 2, 4, 6, 7, 5, 3, 1] if n_col == 8 else list(range(n_col))
    forward, backward = n_col // 2, (n_col - 1) // 2
    jobs = [(0, 0, width)] + [(j, q, rows) for j in range(1, chips) for q in range(CHUNKS)]

    def to_sibling(value):
        return lax.ppermute(value, "row", [(r, r ^ 1) for r in range(n_row)])

    def to_chip(value, shift):
        pairs = [(r, (r + CORES * shift) % n_row) for r in range(n_row)]
        return lax.ppermute(value, "row", pairs)

    def around(value, step):
        pairs = [(ring[i], ring[(i + step) % n_col]) for i in range(n_col)]
        return lax.ppermute(value, "col", pairs)

    def after(value, *others):
        return lax.optimization_barrier((value, others))[0]

    table = []
    for r in range(n_row):
        for c in range(n_col):
            p, x, k = ring.index(c), r // CORES, r % CORES
            entry = [k, int(c == 0), r, r ^ 1]
            for s in range(1, chips):
                there = (x - s) % chips
                entry += [CORES * there + k, CORES * there + 1 - k]
            order = [p] + [p - s for s in range(1, forward + 1)]
            order += [p + s for s in range(1, backward + 1)]
            blocks_at = len(entry)
            entry += [ring[i % n_col] for i in order]
            starts_at = len(entry)
            entry += [((x + j) % chips * width + q * rows) // 16 for j, q, _ in jobs]
            sends_at = len(entry)
            entry += [
                ((x + s + j) % chips * width + q * rows) // 16
                for j, q, _ in jobs for s in range(1, chips)
            ]
            order_at = len(entry)
            for j, q, size in jobs:
                first = ((x + j) % chips * CHUNKS + q) * TILES
                entry += [first + t for t in range(size * TILES // rows)]
            table.append(entry)
    flat = lax.axis_index("row") * n_col + lax.axis_index("col")
    where = lax.dynamic_index_in_dim(np.array(table, np.int32), flat, 0, False)
    rows_at = 2

    mine, other = low_partial(where, activations, basis)
    mine = mine + to_sibling(other)
    mine = encode(mine, *[to_chip(mine, s) for s in range(1, chips)])

    grads = out_grads.T
    moment = after(col_moment, mine)[:, None]
    if pad:
        grads = jnp.pad(grads, ((0, pad), (0, 0)))
        moment = jnp.pad(moment, ((0, pad), (0, 0)), constant_values=1.0)
    grads = after(grads, other)
    sends = cut(where, grads, [size for _, _, size in jobs for _ in range(1, chips)], sends_at)
    sends = [sends[n * (chips - 1) : (n + 1) * (chips - 1)] for n in range(len(jobs))]
    sibling = to_sibling(after(grads, mine))
    moments = after(row_moment, mine)[None]
    moments = [moments, to_sibling(moments)]

    def exchange(job, *others):
        return [to_chip(after(value, *others), s) for s, value in enumerate(sends[job], 1)]

    def pass_on(got, *others):
        got = [after(value, *others) for value in got]
        return [both for value in got for both in (value, to_sibling(value))]

    ahead, behind, other_ahead, other_behind = [mine], [mine], [], []
    got = [exchange(0, mine)]
    for hop in range(forward):
        moving = [around(ahead[-1], 1)]
        if hop < backward:
            moving.append(around(behind[-1], -1))
        passing = [to_sibling(ahead[-1])] + ([to_sibling(behind[-1])] if hop else [])
        extra = got[0] if hop == forward - 1 else []
        if hop == 1:
            turned = turn_basis(after(basis, *ahead))
            extra = [*turned]
        moved = lax.optimization_barrier((*moving, *passing, *extra))
        ahead.append(moved[0])
        behind += moved[1 : len(moving)]
        other_ahead.append(moved[len(moving)])
        other_behind += moved[len(moving) + 1 : len(moving) + len(passing)]
        if hop == forward - 1:
            passed = [pass_on(got[0], *moved)]
            got.append(exchange(1, *moved))
    other_ahead.append(to_sibling(ahead[-1]))
    while len(other_behind) < backward:
        other_behind.append(to_sibling(behind[len(other_behind) + 1]))
    high, low = assemble(where, ahead + behind[1:], other_ahead + other_behind, blocks_at)

    found = []

    def project_job(job, most):
        part, col_next, sums, top = project(
            where, high, low, moment, most, [grads, sibling] + passed[job],
            [] if job else moments, jobs[job][2], rows, starts_at + job, rows_at,
            0.0 if job else hidden * beta_two / (1.0 - beta_two),
        )
        found.append((part, col_next))
        return sums, top

    sums, top = project_job(0, jnp.zeros((1, rank), f32))
    sums = after(sums, *got[1])
    sums = sum((to_chip(sums, s) for s in range(1, chips)), sums)
    passed.append(pass_on(got[1], sums))
    for job in range(2, len(jobs)):
        got.append(exchange(job, sums))
    step, job = 1, 1
    while step < n_col:
        arrived = lax.ppermute(sums, "col", [(c, c ^ step) for c in range(n_col)])
        if step > 1 and job < len(jobs):
            _, top = project_job(job, top)
            arrived, top = lax.optimization_barrier((arrived, top))
            job += 1
        sums = sums + arrived
        if step == 2:
            for n in range(2, len(jobs)):
                passed.append(pass_on(got[n], sums))
        step *= 2
    while job < len(jobs):
        _, top = project_job(job, top)
        job += 1

    updated, row_next, col_next = update(
        where, sums, top, *turned, [part for part, _ in found], [col for _, col in found],
        rows, hidden, n_row, rows_at, order_at,
    )
    return (updated[:columns].T, row_next[0], col_next.reshape(-1)[:columns])


def solution(mesh):
    in_specs = (P("col", "row"), P("row", "col"), P("row", None), P("row"), P("col"))
    out_specs = (P("row", "col"), P("row"), P("col"))
    return jax.shard_map(
        functools.partial(per_device, mesh.shape["row"], mesh.shape["col"]),
        mesh=mesh, in_specs=in_specs, out_specs=out_specs, check_vma=False,
    )
```

```python
import functools

import jax
import jax.numpy as jnp
import numpy as np
from jax import lax
from jax.experimental import pallas as pl
from jax.experimental.pallas import tpu as pltpu
from jax.sharding import PartitionSpec as P

beta_two = 0.8
scale_alpha = 0.25
epsilon = 1e-30
CORES = 2
CHUNKS = 2
HALVES = 2
f32 = jnp.float32
bf16 = jnp.bfloat16
f8 = jnp.float8_e4m3fn
MIB = 1 << 20
CODE_TOP = 181.0
TOP_ROWS = 16
VMEM = pl.BlockSpec(memory_space=pltpu.VMEM)
SMEM = pl.BlockSpec(memory_space=pltpu.SMEM)


def split(value):
    high = value.astype(bf16)
    return high, (value - high.astype(f32)).astype(bf16)


def tile_of(size, most, unit):
    return max(t for t in range(unit, most + 1, unit) if size % t == 0)


def low_kernel(steps, n_col, here_ref, act_ref, basis_ref, mine_ref, other_ref, kept_ref, sem):
    depth = basis_ref.shape[0]
    tile = depth // steps
    half = mine_ref.shape[1]
    copies = []
    for n in range(steps):
        at = pl.ds(n * tile, tile)
        copies.append(pltpu.make_async_copy(basis_ref.at[at, :], kept_ref.at[at, :], sem.at[n]))
    for copy in copies:
        copy.start()
    total = None
    for n in range(steps):
        copies[n].wait()
        at = slice(n * tile, (n + 1) * tile)
        high, low = split(kept_ref[at, :])
        left = act_ref[:, at]
        one = jnp.dot(left, high, preferred_element_type=f32)
        one = one + jnp.dot(left, low, preferred_element_type=f32)
        total = one if total is None else total + one
    second = here_ref[0] // n_col % CORES == 1
    mine_ref[...] = jnp.where(second, total[:, half:], total[:, :half])
    other_ref[...] = jnp.where(second, total[:, :half], total[:, half:])


def low_partial(here, acts, basis, n_col):
    tokens, depth = acts.shape
    rank = basis.shape[1]
    steps = 8
    half = jax.ShapeDtypeStruct((tokens, rank // 2), f32)
    return pl.pallas_call(
        functools.partial(low_kernel, steps, n_col),
        out_shape=(half, half),
        grid_spec=pltpu.PrefetchScalarGridSpec(
            num_scalar_prefetch=1,
            grid=(1,),
            in_specs=[
                pl.BlockSpec((tokens, depth), lambda i, s: (0, 0)),
                pl.BlockSpec(memory_space=pl.ANY),
            ],
            out_specs=[VMEM] * 2,
            scratch_shapes=[
                pltpu.VMEM((depth, rank), f32),
                pltpu.SemaphoreType.DMA((steps,)),
            ],
        ),
        compiler_params=pltpu.CompilerParams(vmem_limit_bytes=60 * MIB),
        cost_estimate=pl.CostEstimate(
            flops=4 * tokens * depth * rank, bytes_accessed=6 * depth * rank, transcendentals=0
        ),
        name="low_partial",
    )(here, acts, basis)


def turn_kernel(basis_ref, high_ref, small_ref):
    rows, rank = basis_ref.shape
    tile = tile_of(rows, 256, 128)
    for begin in range(0, rows, tile):
        at = slice(begin, begin + tile)
        turned = basis_ref[at, :].T
        high = turned.astype(bf16)
        high_ref[:, at] = high
        small_ref[:rank, at] = ((turned - high.astype(f32)) * 2.0**20).astype(f8)
        small_ref[rank:, at] = (turned * 2.0**12).astype(f8)


def turn_basis(basis):
    rows, rank = basis.shape
    return pl.pallas_call(
        turn_kernel,
        out_shape=[
            jax.ShapeDtypeStruct((rank, rows), bf16),
            jax.ShapeDtypeStruct((2 * rank, rows), f8),
        ],
        in_specs=[VMEM],
        out_specs=[VMEM] * 2,
        compiler_params=pltpu.CompilerParams(vmem_limit_bytes=4 * MIB),
        cost_estimate=pl.CostEstimate(flops=0, bytes_accessed=8 * rows * rank, transcendentals=0),
        name="turn_basis",
    )(basis)


def encode_kernel(*refs):
    out_ref = refs[-1]
    tokens, lanes = refs[0].shape
    value = refs[0][...]
    for ref in refs[1:-1]:
        value = value + ref[...]
    size = jnp.abs(value)
    top = (jnp.max(size, axis=0, keepdims=True) * (1.0 + 2.0**-7)).astype(bf16).astype(f32)
    top = jnp.maximum(top, 1e-36)
    code = size * (CODE_TOP / top)
    for _ in range(4):
        code = code * code
    out_ref[:tokens, :] = jnp.where(value < 0, -code, code).astype(bf16)
    out_ref[tokens:, :] = jnp.broadcast_to(top, (TOP_ROWS, lanes)).astype(bf16)


def encode(*blocks):
    tokens, lanes = blocks[0].shape
    return pl.pallas_call(
        encode_kernel,
        out_shape=jax.ShapeDtypeStruct((tokens + TOP_ROWS, lanes), bf16),
        in_specs=[VMEM] * len(blocks),
        out_specs=VMEM,
        compiler_params=pltpu.CompilerParams(vmem_limit_bytes=4 * MIB),
        cost_estimate=pl.CostEstimate(
            flops=0, bytes_accessed=8 * tokens * lanes, transcendentals=0
        ),
        name="encode",
    )(*blocks)


def decode(ref):
    tokens = ref.shape[0] - TOP_ROWS
    code = ref[:tokens, :].astype(f32)
    size = jnp.abs(code)
    for _ in range(4):
        size = lax.rsqrt(size)
    size = size * (ref[tokens : tokens + 1, :].astype(f32) * (1.0 / CODE_TOP))
    return jnp.where(code < 0, -size, size)


def join_kernel(where_ref, mine_ref, other_ref, out_ref):
    half = mine_ref.shape[1]
    core = where_ref[0]
    out_ref[:, pl.ds(pl.multiple_of(core * half, half), half)] = mine_ref[...]
    out_ref[:, pl.ds(pl.multiple_of((1 - core) * half, half), half)] = other_ref[...]


def join(where, mine, other):
    rows, half = mine.shape
    return pl.pallas_call(
        join_kernel,
        out_shape=jax.ShapeDtypeStruct((rows, 2 * half), bf16),
        in_specs=[SMEM, VMEM, VMEM],
        out_specs=VMEM,
        compiler_params=pltpu.CompilerParams(vmem_limit_bytes=4 * MIB),
        cost_estimate=pl.CostEstimate(flops=0, bytes_accessed=8 * rows * half, transcendentals=0),
        name="join",
    )(where, mine, other)


def assemble_kernel(blocks, offset, where_ref, *refs):
    high_ref, low_ref = refs[blocks:]
    for b, ref in enumerate(refs[:blocks]):
        tokens = ref.shape[0] - TOP_ROWS
        rows = pl.ds(pl.multiple_of(where_ref[offset + b] * tokens, tokens), tokens)
        high_ref[rows, :], low_ref[rows, :] = split(decode(ref))


def assemble(where, found, offset):
    blocks = len(found)
    rows, rank = found[0].shape
    shape = (blocks * (rows - TOP_ROWS), rank)
    return pl.pallas_call(
        functools.partial(assemble_kernel, blocks, offset),
        out_shape=[jax.ShapeDtypeStruct(shape, bf16)] * 2,
        in_specs=[SMEM] + [VMEM] * blocks,
        out_specs=[VMEM] * 2,
        compiler_params=pltpu.CompilerParams(vmem_limit_bytes=4 * MIB),
        cost_estimate=pl.CostEstimate(flops=0, bytes_accessed=0, transcendentals=0),
        name="assemble",
    )(where, *found)


def cut_kernel(starts_at, counts, where_ref, grads_ref, *refs):
    outs, sem = refs[:-1], refs[-1]
    copies = []
    for n, out in enumerate(outs):
        rows = out.shape[0]
        at = pl.ds(pl.multiple_of(where_ref[starts_at + n] * 16, 16), rows)
        copies.append(pltpu.make_async_copy(grads_ref.at[at, :], out, sem.at[n]))
    for copy in copies:
        copy.start()
    for copy in copies:
        copy.wait()


def cut(where, grads, sizes, starts_at):
    return pl.pallas_call(
        functools.partial(cut_kernel, starts_at, len(sizes)),
        out_shape=[jax.ShapeDtypeStruct((size, grads.shape[1]), bf16) for size in sizes],
        in_specs=[SMEM, pl.BlockSpec(memory_space=pl.ANY)],
        out_specs=[VMEM] * len(sizes),
        scratch_shapes=[pltpu.SemaphoreType.DMA((len(sizes),))],
        compiler_params=pltpu.CompilerParams(vmem_limit_bytes=4 * MIB),
        cost_estimate=pl.CostEstimate(
            flops=0, bytes_accessed=4 * sum(sizes) * grads.shape[1], transcendentals=0
        ),
        name="cut",
    )(where, grads)


def project_kernel(
    pieces, skip, step, start_at, rows_at, first, where_ref, high_ref, low_ref, moment_ref,
    most_ref, *refs
):
    out_ref, colnext_ref, sums_ref, top_ref = refs[len(refs) - 4 :]
    grads, moments = refs[:pieces], refs[pieces : len(refs) - 4]
    rows, rank = out_ref.shape
    tokens = grads[0].shape[1]
    order = [
        pl.ds(pl.multiple_of(where_ref[rows_at + p] * tokens, tokens), tokens)
        for p in range(pieces)
    ]
    high = jnp.concatenate([high_ref[at, :] for at in order], axis=0)
    low = jnp.concatenate([low_ref[at, :] for at in order], axis=0)
    sums = jnp.zeros((1, rank), f32)
    if first:
        lanes = moments[0].shape[1]
        owner = lax.broadcasted_iota(jnp.int32, (1, rank), 1) // lanes
        for n, ref in enumerate(moments):
            wide = jnp.concatenate([ref[...]] * (rank // lanes), axis=1)
            sums = jnp.where(owner == where_ref[rows_at + n], wide, sums)
        sums = sums * jnp.where(where_ref[1] == 1, first, 0.0)
    top = most_ref[...]
    for begin in range(0, rows, step):
        at = pl.ds(pl.multiple_of(where_ref[start_at] * 16 + begin, 16), step)
        here = slice(begin, begin + step)
        there = slice(skip + begin, skip + begin + step)
        grad = jnp.concatenate(
            [g[at, :] for g in grads[:2]] + [g[there, :] for g in grads[2:]], axis=1
        )
        total = jnp.dot(grad, high, preferred_element_type=f32) + jnp.dot(
            grad, low, preferred_element_type=f32
        )
        squares = total * total
        sums = sums + jnp.sum(squares, axis=0, keepdims=True)
        quarter = sum(squares[:, n : n + 128] for n in range(0, rank, 128))
        col_next = beta_two * moment_ref[at, :] + (1.0 - beta_two) * (
            jnp.sum(quarter, axis=1, keepdims=True) / rank + epsilon
        )
        part = total * lax.rsqrt(col_next)
        top = jnp.maximum(top, jnp.max(jnp.abs(part), axis=0, keepdims=True))
        out_ref[here, :] = part
        long = colnext_ref.shape[1]
        wide = jnp.broadcast_to(col_next, (step, 128))
        if long > step:
            wide = jnp.concatenate([wide, jnp.zeros((long - step, 128), f32)], axis=0)
        colnext_ref[begin // step : begin // step + 1, :] = wide.T[:1, :]
    sums_ref[...] = sums
    top_ref[...] = top


def project(
    where, high, low, moment, most, grads, skip, moments, rows, step, start_at, rows_at, first
):
    tokens, rank = high.shape
    long = -(-step // 128) * 128
    return pl.pallas_call(
        functools.partial(
            project_kernel, len(grads), skip, step, start_at, rows_at, first
        ),
        out_shape=[
            jax.ShapeDtypeStruct((rows, rank), f32),
            jax.ShapeDtypeStruct((rows // step, long), f32),
            jax.ShapeDtypeStruct((1, rank), f32),
            jax.ShapeDtypeStruct((1, rank), f32),
        ],
        in_specs=[SMEM] + [VMEM] * (4 + len(grads) + len(moments)),
        out_specs=[VMEM] * 4,
        compiler_params=pltpu.CompilerParams(vmem_limit_bytes=16 * MIB),
        cost_estimate=pl.CostEstimate(flops=0, bytes_accessed=0, transcendentals=0),
        name="project",
    )(where, high, low, moment, most, *grads, *moments)


def segments(refs, part_refs, tile):
    found, done = [], 0
    for ref, part_ref in zip(refs, part_refs):
        rows = part_ref.shape[0]
        for row in range(0, rows, tile):
            size = min(tile, rows - row)
            found.append((done // tile, done % tile, size, ref, row))
            done += size
    return found


def update_kernel(
    count, parts, rows_at, order_at, where_ref, sums_ref, most_ref, high_ref, small_ref, *refs
):
    part_refs, col_refs = refs[:parts], refs[parts : 2 * parts]
    out_ref, rownext_ref, colnext_ref, lhs_ref, lhs_small_ref, scale_ref = refs[2 * parts :]
    tiles, tile, rank = lhs_ref.shape
    step = pl.program_id(0)

    @pl.when(step == 0)
    def _():
        row_next = (1.0 - beta_two) * (sums_ref[...] / count + epsilon)
        rows = rownext_ref.shape[1]
        held = jnp.zeros((1, rows), f32)
        for r in range(rank // rows):
            held = jnp.where(where_ref[rows_at] == r, row_next[:, r * rows : (r + 1) * rows], held)
        rownext_ref[...] = held
        scale = scale_alpha * lax.rsqrt(row_next) * jnp.sqrt(
            jnp.mean(row_next, axis=1, keepdims=True)
        )
        strip = colnext_ref.shape[1]
        for n, begin, size, ref, row in segments(col_refs, part_refs, tile):
            strip = pl.ds(where_ref[order_at + n], 1)
            colnext_ref[strip, begin : begin + size] = ref[row // tile : row // tile + 1, :size]
        top = jnp.maximum(jnp.max(scale * most_ref[...], axis=1, keepdims=True), 1e-30)
        scale_ref[0:1, :] = scale
        scale_ref[1:2, :] = jnp.broadcast_to(2.0**7 / top, (1, rank))
        scale_ref[2:3, :] = jnp.broadcast_to(top * 2.0**-27, (1, rank))

    for number in range(tiles):

        @pl.when(step == number)
        def _():
            for n, begin, size, ref, row in segments(part_refs, part_refs, tile):
                if n != number:
                    continue
                value = ref[row : row + size, :] * scale_ref[0:1, :]
                high = value.astype(bf16)
                grow = scale_ref[1:2, :]
                at = slice(begin, begin + size)
                lhs_ref[number, at, :] = high
                lhs_small_ref[number, at, :rank] = (value * grow).astype(f8)
                lhs_small_ref[number, at, rank:] = (
                    (value - high.astype(f32)) * (grow * 2.0**8)
                ).astype(f8)

    now = step % tiles
    lanes = pl.ds(pl.multiple_of(step // tiles * out_ref.shape[1], 128), out_ref.shape[1])
    out_ref[...] = jnp.dot(
        lhs_ref[now], high_ref[:, lanes], preferred_element_type=f32
    ) + scale_ref[2:3, 0:1] * jnp.dot(
        lhs_small_ref[now], small_ref[:, lanes], preferred_element_type=f32
    )


def update(where, sums, most, high, small, parts, cols, strip, hidden, n_row, rows_at, order_at):
    rank, rows = high.shape
    columns = sum(part.shape[0] for part in parts)
    tiles = columns // strip
    wide = rows // HALVES
    return pl.pallas_call(
        functools.partial(update_kernel, float(hidden), len(parts), rows_at, order_at),
        out_shape=[
            jax.ShapeDtypeStruct((columns, rows), f32),
            jax.ShapeDtypeStruct((1, rank // n_row), f32),
            jax.ShapeDtypeStruct((tiles, strip), f32),
        ],
        grid_spec=pltpu.PrefetchScalarGridSpec(
            num_scalar_prefetch=1,
            grid=(tiles * HALVES,),
            in_specs=[VMEM] * (4 + 2 * len(parts)),
            out_specs=[
                pl.BlockSpec((strip, wide), lambda i, s: (s[order_at + i % tiles], i // tiles)),
                pl.BlockSpec((1, rank // n_row), lambda i, s: (0, 0)),
                pl.BlockSpec((tiles, strip), lambda i, s: (0, 0)),
            ],
            scratch_shapes=[
                pltpu.VMEM((tiles, strip, rank), bf16),
                pltpu.VMEM((tiles, strip, 2 * rank), f8),
                pltpu.VMEM((8, rank), f32),
            ],
        ),
        compiler_params=pltpu.CompilerParams(vmem_limit_bytes=28 * MIB),
        cost_estimate=pl.CostEstimate(
            flops=4 * columns * rank * rows, bytes_accessed=4 * columns * rows, transcendentals=0
        ),
        name="update",
    )(where, sums, most, high, small, *parts, *cols)


def per_device(n_row, n_col, activations, out_grads, basis, row_moment, col_moment):
    chips = n_row // CORES
    columns = col_moment.shape[0]
    hidden = columns * n_col
    rank = basis.shape[1]
    width = -(-columns // (32 * chips)) * 32
    pad = width * chips - columns
    rows = width // CHUNKS
    ring = [0, 2, 4, 6, 7, 5, 3, 1] if n_col == 8 else list(range(n_col))
    hops = n_col // 2
    jobs, moves = [(0, 0, width, 0, 0)], [(0, 0, width)]
    for j in range(1, chips):
        for q in range(CHUNKS):
            at, part = q * rows, rows * (3 - q) // 5 // 128 * 128
            if j > 1 or part == 0:
                jobs.append((j, at, rows, len(moves), 0))
                moves.append((j, at, rows))
                continue
            jobs.append((j, at, part, len(moves), 0))
            if q == 0:
                jobs.append((j, at + part, rows - part, len(moves), part))
                moves.append((j, at, rows))
            else:
                jobs.append((j, at + part, rows - part, len(moves) + 1, 0))
                moves += [(j, at, part), (j, at + part, rows - part)]

    def to_sibling(value):
        return lax.ppermute(value, "row", [(r, r ^ 1) for r in range(n_row)])

    def to_chip(value, shift):
        pairs = [(r, (r + CORES * shift) % n_row) for r in range(n_row)]
        return lax.ppermute(value, "row", pairs)

    def around(value):
        pairs = [
            (r * n_col + ring[i], r * n_col + ring[(i + 1 - r % CORES * 2) % n_col])
            for r in range(n_row) for i in range(n_col)
        ]
        return lax.ppermute(value, ("row", "col"), pairs)

    def after(value, *others):
        return lax.optimization_barrier((value, others))[0]

    table = []
    for r in range(n_row):
        for c in range(n_col):
            p, x, k = ring.index(c), r // CORES, r % CORES
            entry = [k, int(c == 0), r, r ^ 1]
            for s in range(1, chips):
                there = (x - s) % chips
                entry += [CORES * there + k, CORES * there + 1 - k]
            way = 1 - 2 * k
            order = [p] + [p - way * s for s in range(1, hops + 1)]
            order += [p + way * s for s in range(1, hops + 1) if 2 * s != n_col]
            blocks_at = len(entry)
            entry += [ring[i % n_col] for i in order]
            starts_at = len(entry)
            entry += [((x + j) % chips * width + at) // 16 for j, at, *_ in jobs]
            sends_at = len(entry)
            entry += [
                ((x + s + j) % chips * width + at) // 16
                for j, at, _ in moves for s in range(1, chips)
            ]
            order_at = len(entry)
            entry += [(x + j) % chips * CHUNKS + q for j in range(chips) for q in range(CHUNKS)]
            table.append(entry)
    flat = lax.axis_index("row") * n_col + lax.axis_index("col")
    here = flat.astype(jnp.int32)[None]
    rows_at = 2

    mine, other = low_partial(here, activations, basis, n_col)
    table = np.array(table, np.int32)
    flat = after(flat.astype(jnp.uint32), other)
    where = lax.dynamic_slice(table, (flat, jnp.uint32(0)), (1, table.shape[1]))[0]
    mine = mine + to_sibling(other)
    arrived = [to_chip(mine, s) for s in range(1, chips)]

    grads = out_grads.T
    moment = after(col_moment, mine)[:, None]
    if pad:
        grads = jnp.pad(grads, ((0, pad), (0, 0)))
        moment = jnp.pad(moment, ((0, pad), (0, 0)), constant_values=1.0)
    grads = after(grads, other)
    sends = cut(where, grads, [size for _, _, size in moves for _ in range(1, chips)], sends_at)
    arrived = lax.optimization_barrier((*arrived, *sends))
    sends, arrived = arrived[chips - 1 :], arrived[: chips - 1]
    sends = [sends[n * (chips - 1) : (n + 1) * (chips - 1)] for n in range(len(moves))]
    mine = encode(mine, *arrived)
    moments = after(row_moment, mine)[None]
    moments = [moments, to_sibling(moments)]

    def exchange(send, *others):
        return [to_chip(after(value, *others), s) for s, value in enumerate(sends[send], 1)]

    def pass_on(got, *others):
        got = [after(value, *others) for value in got]
        return [both for value in got for both in (value, to_sibling(value))]

    got = {0: exchange(0, mine)}
    held = join(where, mine, to_sibling(mine))
    sibling = to_sibling(after(grads, held))
    blocks, siblings = [held], []
    for hop in range(1, hops + 1):
        moving = [around(held)]
        if hop > 1:
            moving.append(to_sibling(held))
        if hop == 2:
            turned = turn_basis(after(basis, held))
            moving += turned
        if hop == max(hops - 1, 1):
            moving += got[0]
        moved = lax.optimization_barrier(tuple(moving))
        held = moved[0]
        blocks.append(held)
        siblings += moved[1:2] if hop > 1 else []
        if hop == max(hops - 1, 1):
            passed = {0: pass_on(got[0], held)}
            for move in (1, 2):
                got[move] = exchange(move, held)
    if 2 * hops != n_col:
        siblings.append(to_sibling(held))
    high, low = assemble(where, blocks + siblings, blocks_at)

    found = []

    def project_job(job, most):
        _, _, size, move, skip = jobs[job]
        part, col_next, sums, top = project(
            where, high, low, moment, most, [grads, sibling] + passed[move], skip,
            [] if job else moments, size, min(size, rows), starts_at + job, rows_at,
            0.0 if job else hidden * beta_two / (1.0 - beta_two),
        )
        found.append((part, col_next))
        return sums, top

    sums, top = project_job(0, jnp.zeros((1, rank), f32))
    sums = after(sums, *got[1], *got[2])
    passed[1] = pass_on(got[1], sums)
    hop, step = 0, 1
    while step < n_col:
        if hop == 0:
            arrived = [to_chip(sums, s) for s in range(1, chips)]
        else:
            arrived = [lax.ppermute(sums, "col", [(c, c ^ step) for c in range(n_col)])]
            step *= 2
        hop += 1
        if hop < len(jobs) and jobs[hop][3] in passed:
            _, top = project_job(hop, top)
            *arrived, top = lax.optimization_barrier((*arrived, top))
        sums = sum(arrived, sums)
        if hop == 1:
            passed[2] = pass_on(got[2], sums)
            for move in range(3, len(moves)):
                got[move] = exchange(move, sums)
        if hop == 3:
            for move in range(3, len(moves)):
                passed[move] = pass_on(got[move], sums)
    for job in range(len(found), len(jobs)):
        _, top = project_job(job, top)

    updated, row_next, col_next = update(
        where, sums, top, *turned, [part for part, _ in found], [col for _, col in found],
        rows, hidden, n_row, rows_at, order_at,
    )
    return (updated[:columns].T, row_next[0], col_next.reshape(-1)[:columns])


def solution(mesh):
    in_specs = (P("col", "row"), P("row", "col"), P("row", None), P("row"), P("col"))
    out_specs = (P("row", "col"), P("row"), P("col"))
    return jax.shard_map(
        functools.partial(per_device, mesh.shape["row"], mesh.shape["col"]),
        mesh=mesh, in_specs=in_specs, out_specs=out_specs, check_vma=False,
    )
```

```python
import functools

import jax
import jax.numpy as jnp
import numpy as np
from jax import lax
from jax.experimental import pallas as pl
from jax.experimental.pallas import tpu as pltpu
from jax.sharding import PartitionSpec as P

beta_two = 0.8
scale_alpha = 0.25
epsilon = 1e-30
CORES = 2
CHUNKS = 2
HALVES = 2
f32 = jnp.float32
bf16 = jnp.bfloat16
f8 = jnp.float8_e4m3fn
MIB = 1 << 20
CODE_TOP = 181.0
TOP_ROWS = 16
VMEM = pl.BlockSpec(memory_space=pltpu.VMEM)
SMEM = pl.BlockSpec(memory_space=pltpu.SMEM)


def split(value):
    high = value.astype(bf16)
    return high, (value - high.astype(f32)).astype(bf16)


def tile_of(size, most, unit):
    return max(t for t in range(unit, most + 1, unit) if size % t == 0)


def low_kernel(steps, n_col, here_ref, act_ref, basis_ref, mine_ref, other_ref, kept_ref, sem):
    depth = basis_ref.shape[0]
    tile = depth // steps
    half = mine_ref.shape[1]
    copies = []
    for n in range(steps):
        at = pl.ds(n * tile, tile)
        copies.append(pltpu.make_async_copy(basis_ref.at[at, :], kept_ref.at[at, :], sem.at[n]))
    for copy in copies:
        copy.start()
    total = None
    for n in range(steps):
        copies[n].wait()
        at = slice(n * tile, (n + 1) * tile)
        high, low = split(kept_ref[at, :])
        left = act_ref[:, at]
        one = jnp.dot(left, high, preferred_element_type=f32)
        one = one + jnp.dot(left, low, preferred_element_type=f32)
        total = one if total is None else total + one
    second = here_ref[0] // n_col % CORES == 1
    mine_ref[...] = jnp.where(second, total[:, half:], total[:, :half])
    other_ref[...] = jnp.where(second, total[:, :half], total[:, half:])


def low_partial(here, acts, basis, n_col):
    tokens, depth = acts.shape
    rank = basis.shape[1]
    steps = 8
    half = jax.ShapeDtypeStruct((tokens, rank // 2), f32)
    return pl.pallas_call(
        functools.partial(low_kernel, steps, n_col),
        out_shape=(half, half),
        grid_spec=pltpu.PrefetchScalarGridSpec(
            num_scalar_prefetch=1,
            grid=(1,),
            in_specs=[
                pl.BlockSpec((tokens, depth), lambda i, s: (0, 0)),
                pl.BlockSpec(memory_space=pl.ANY),
            ],
            out_specs=[VMEM] * 2,
            scratch_shapes=[
                pltpu.VMEM((depth, rank), f32),
                pltpu.SemaphoreType.DMA((steps,)),
            ],
        ),
        compiler_params=pltpu.CompilerParams(vmem_limit_bytes=60 * MIB),
        cost_estimate=pl.CostEstimate(
            flops=4 * tokens * depth * rank, bytes_accessed=6 * depth * rank, transcendentals=0
        ),
        name="low_partial",
    )(here, acts, basis)


def turn_kernel(basis_ref, high_ref, small_ref):
    rows, rank = basis_ref.shape
    tile = tile_of(rows, 256, 128)
    for begin in range(0, rows, tile):
        at = slice(begin, begin + tile)
        turned = basis_ref[at, :].T
        high = turned.astype(bf16)
        high_ref[:, at] = high
        small_ref[:rank, at] = ((turned - high.astype(f32)) * 2.0**20).astype(f8)
        small_ref[rank:, at] = (turned * 2.0**12).astype(f8)


def turn_basis(basis):
    rows, rank = basis.shape
    return pl.pallas_call(
        turn_kernel,
        out_shape=[
            jax.ShapeDtypeStruct((rank, rows), bf16),
            jax.ShapeDtypeStruct((2 * rank, rows), f8),
        ],
        in_specs=[VMEM],
        out_specs=[VMEM] * 2,
        compiler_params=pltpu.CompilerParams(vmem_limit_bytes=4 * MIB),
        cost_estimate=pl.CostEstimate(flops=0, bytes_accessed=8 * rows * rank, transcendentals=0),
        name="turn_basis",
    )(basis)


def encode_kernel(*refs):
    out_ref = refs[-1]
    tokens, lanes = refs[0].shape
    value = refs[0][...]
    for ref in refs[1:-1]:
        value = value + ref[...]
    size = jnp.abs(value)
    top = (jnp.max(size, axis=0, keepdims=True) * (1.0 + 2.0**-7)).astype(bf16).astype(f32)
    top = jnp.maximum(top, 1e-36)
    code = size * (CODE_TOP / top)
    for _ in range(4):
        code = code * code
    out_ref[:tokens, :] = jnp.where(value < 0, -code, code).astype(bf16)
    out_ref[tokens:, :] = jnp.broadcast_to(top, (TOP_ROWS, lanes)).astype(bf16)


def encode(*blocks):
    tokens, lanes = blocks[0].shape
    return pl.pallas_call(
        encode_kernel,
        out_shape=jax.ShapeDtypeStruct((tokens + TOP_ROWS, lanes), bf16),
        in_specs=[VMEM] * len(blocks),
        out_specs=VMEM,
        compiler_params=pltpu.CompilerParams(vmem_limit_bytes=4 * MIB),
        cost_estimate=pl.CostEstimate(
            flops=0, bytes_accessed=8 * tokens * lanes, transcendentals=0
        ),
        name="encode",
    )(*blocks)


def decode(ref):
    tokens = ref.shape[0] - TOP_ROWS
    code = ref[:tokens, :].astype(f32)
    size = jnp.abs(code)
    for _ in range(4):
        size = lax.rsqrt(size)
    size = size * (ref[tokens : tokens + 1, :].astype(f32) * (1.0 / CODE_TOP))
    return jnp.where(code < 0, -size, size)


def join_kernel(where_ref, mine_ref, other_ref, out_ref):
    half = mine_ref.shape[1]
    core = where_ref[0]
    out_ref[:, pl.ds(pl.multiple_of(core * half, half), half)] = mine_ref[...]
    out_ref[:, pl.ds(pl.multiple_of((1 - core) * half, half), half)] = other_ref[...]


def join(where, mine, other):
    rows, half = mine.shape
    return pl.pallas_call(
        join_kernel,
        out_shape=jax.ShapeDtypeStruct((rows, 2 * half), bf16),
        in_specs=[SMEM, VMEM, VMEM],
        out_specs=VMEM,
        compiler_params=pltpu.CompilerParams(vmem_limit_bytes=4 * MIB),
        cost_estimate=pl.CostEstimate(flops=0, bytes_accessed=8 * rows * half, transcendentals=0),
        name="join",
    )(where, mine, other)


def assemble_kernel(offsets, where_ref, *refs):
    high_ref, low_ref = refs[len(refs) - 2 :]
    for offset, ref in zip(offsets, refs):
        tokens = ref.shape[0] - TOP_ROWS
        rows = pl.ds(pl.multiple_of(where_ref[offset] * tokens, tokens), tokens)
        high_ref[rows, :], low_ref[rows, :] = split(decode(ref))


def assemble(where, found, offsets, tokens, previous=()):
    rank = found[0].shape[1]
    first = 1 + len(found)
    return pl.pallas_call(
        functools.partial(assemble_kernel, offsets),
        out_shape=[jax.ShapeDtypeStruct((tokens, rank), bf16)] * 2,
        in_specs=[SMEM] + [VMEM] * (len(found) + len(previous)),
        out_specs=[VMEM] * 2,
        input_output_aliases={first + n: n for n in range(len(previous))},
        compiler_params=pltpu.CompilerParams(vmem_limit_bytes=4 * MIB),
        cost_estimate=pl.CostEstimate(
            flops=0,
            bytes_accessed=0 if previous else 8 * tokens * rank,
            transcendentals=0,
        ),
        name="assemble",
    )(where, *found, *previous)


def cut_kernel(starts_at, counts, where_ref, grads_ref, *refs):
    outs, sem = refs[:-1], refs[-1]
    copies = []
    for n, out in enumerate(outs):
        rows = out.shape[0]
        at = pl.ds(pl.multiple_of(where_ref[starts_at + n] * 16, 16), rows)
        copies.append(pltpu.make_async_copy(grads_ref.at[at, :], out, sem.at[n]))
    for copy in copies:
        copy.start()
    for copy in copies:
        copy.wait()


def cut(where, grads, sizes, starts_at):
    return pl.pallas_call(
        functools.partial(cut_kernel, starts_at, len(sizes)),
        out_shape=[jax.ShapeDtypeStruct((size, grads.shape[1]), bf16) for size in sizes],
        in_specs=[SMEM, pl.BlockSpec(memory_space=pl.ANY)],
        out_specs=[VMEM] * len(sizes),
        scratch_shapes=[pltpu.SemaphoreType.DMA((len(sizes),))],
        compiler_params=pltpu.CompilerParams(vmem_limit_bytes=4 * MIB),
        cost_estimate=pl.CostEstimate(
            flops=0, bytes_accessed=4 * sum(sizes) * grads.shape[1], transcendentals=0
        ),
        name="cut",
    )(where, grads)


def project_kernel(
    pieces, skip, step, start_at, rows_at, first, where_ref, high_ref, low_ref, moment_ref,
    most_ref, *refs
):
    out_ref, colnext_ref, sums_ref, top_ref = refs[len(refs) - 4 :]
    grads, moments = refs[:pieces], refs[pieces : len(refs) - 4]
    rows, rank = out_ref.shape
    tokens = grads[0].shape[1]
    order = [
        pl.ds(pl.multiple_of(where_ref[rows_at + p] * tokens, tokens), tokens)
        for p in range(pieces)
    ]
    high = jnp.concatenate([high_ref[at, :] for at in order], axis=0)
    low = jnp.concatenate([low_ref[at, :] for at in order], axis=0)
    sums = jnp.zeros((1, rank), f32)
    if first:
        lanes = moments[0].shape[1]
        owner = lax.broadcasted_iota(jnp.int32, (1, rank), 1) // lanes
        for n, ref in enumerate(moments):
            wide = jnp.concatenate([ref[...]] * (rank // lanes), axis=1)
            sums = jnp.where(owner == where_ref[rows_at + n], wide, sums)
        sums = sums * jnp.where(where_ref[1] == 1, first, 0.0)
    top = most_ref[...]
    for begin in range(0, rows, step):
        at = pl.ds(pl.multiple_of(where_ref[start_at] * 16 + begin, 16), step)
        here = slice(begin, begin + step)
        there = slice(skip + begin, skip + begin + step)
        grad = jnp.concatenate(
            [g[at, :] for g in grads[:2]] + [g[there, :] for g in grads[2:]], axis=1
        )
        total = jnp.dot(grad, high, preferred_element_type=f32) + jnp.dot(
            grad, low, preferred_element_type=f32
        )
        squares = total * total
        sums = sums + jnp.sum(squares, axis=0, keepdims=True)
        quarter = sum(squares[:, n : n + 128] for n in range(0, rank, 128))
        col_next = beta_two * moment_ref[at, :] + (1.0 - beta_two) * (
            jnp.sum(quarter, axis=1, keepdims=True) / rank + epsilon
        )
        part = total * lax.rsqrt(col_next)
        top = jnp.maximum(top, jnp.max(jnp.abs(part), axis=0, keepdims=True))
        out_ref[here, :] = part
        long = colnext_ref.shape[1]
        wide = jnp.broadcast_to(col_next, (step, 128))
        if long > step:
            wide = jnp.concatenate([wide, jnp.zeros((long - step, 128), f32)], axis=0)
        colnext_ref[begin // step : begin // step + 1, :] = wide.T[:1, :]
    sums_ref[...] = sums
    top_ref[...] = top


def project(
    where, high, low, moment, most, grads, skip, moments, rows, step, start_at, rows_at, first
):
    tokens, rank = high.shape
    long = -(-step // 128) * 128
    return pl.pallas_call(
        functools.partial(
            project_kernel, len(grads), skip, step, start_at, rows_at, first
        ),
        out_shape=[
            jax.ShapeDtypeStruct((rows, rank), f32),
            jax.ShapeDtypeStruct((rows // step, long), f32),
            jax.ShapeDtypeStruct((1, rank), f32),
            jax.ShapeDtypeStruct((1, rank), f32),
        ],
        in_specs=[SMEM] + [VMEM] * (4 + len(grads) + len(moments)),
        out_specs=[VMEM] * 4,
        compiler_params=pltpu.CompilerParams(vmem_limit_bytes=16 * MIB),
        cost_estimate=pl.CostEstimate(flops=0, bytes_accessed=0, transcendentals=0),
        name="project",
    )(where, high, low, moment, most, *grads, *moments)


def segments(refs, part_refs, tile):
    found, done = [], 0
    for ref, part_ref in zip(refs, part_refs):
        rows = part_ref.shape[0]
        for row in range(0, rows, tile):
            size = min(tile, rows - row)
            found.append((done // tile, done % tile, size, ref, row))
            done += size
    return found


def update_kernel(
    count, parts, rows_at, order_at, where_ref, sums_ref, most_ref, high_ref, small_ref, *refs
):
    part_refs, col_refs = refs[:parts], refs[parts : 2 * parts]
    out_ref, rownext_ref, colnext_ref, lhs_ref, lhs_small_ref, slot_ref, sem = refs[2 * parts :]
    tiles, tile, rank = lhs_ref.shape
    wide = slot_ref.shape[2]
    row_next = (1.0 - beta_two) * (sums_ref[...] / count + epsilon)
    scale = scale_alpha * lax.rsqrt(row_next) * jnp.sqrt(
        jnp.mean(row_next, axis=1, keepdims=True)
    )
    top = jnp.maximum(jnp.max(scale * most_ref[...], axis=1, keepdims=True), 1e-30)
    grow = scale * (2.0**7 / top)
    shrink = top * 2.0**-27

    def prepare(number):
        for n, begin, size, ref, row in segments(part_refs, part_refs, tile):
            if n != number:
                continue
            part = ref[row : row + size, :]
            value = part * scale
            high = value.astype(bf16)
            at = slice(begin, begin + size)
            lhs_ref[number, at, :] = high
            lhs_small_ref[number, at, :rank] = (part * grow).astype(f8)
            lhs_small_ref[number, at, rank:] = (
                (value - high.astype(f32)) * (2.0**15 / top)
            ).astype(f8)

    prepare(0)
    copies = [None, None]
    for number in range(tiles):
        strip = pl.ds(pl.multiple_of(where_ref[order_at + number] * tile, 8), tile)
        for half in range(HALVES):
            slot = (number * HALVES + half) % 2
            lanes = slice(half * wide, (half + 1) * wide)
            if copies[slot] is not None:
                copies[slot].wait()
            if half == 0 and number + 1 < tiles:
                prepare(number + 1)
            slot_ref[slot] = jnp.dot(
                lhs_ref[number], high_ref[:, lanes], preferred_element_type=f32
            ) + shrink * jnp.dot(
                lhs_small_ref[number], small_ref[:, lanes], preferred_element_type=f32
            )
            copies[slot] = pltpu.make_async_copy(
                slot_ref.at[slot], out_ref.at[strip, pl.ds(half * wide, wide)], sem.at[slot]
            )
            copies[slot].start()

    rows = rownext_ref.shape[1]
    held = jnp.zeros((1, rows), f32)
    for r in range(rank // rows):
        held = jnp.where(where_ref[rows_at] == r, row_next[:, r * rows : (r + 1) * rows], held)
    rownext_ref[...] = held
    for n, begin, size, ref, row in segments(col_refs, part_refs, tile):
        strip = pl.ds(where_ref[order_at + n], 1)
        colnext_ref[strip, begin : begin + size] = ref[row // tile : row // tile + 1, :size]
    for copy in copies:
        copy.wait()


def update(where, sums, most, high, small, parts, cols, strip, hidden, n_row, rows_at, order_at):
    rank, rows = high.shape
    columns = sum(part.shape[0] for part in parts)
    tiles = columns // strip
    return pl.pallas_call(
        functools.partial(update_kernel, float(hidden), len(parts), rows_at, order_at),
        out_shape=[
            jax.ShapeDtypeStruct((columns, rows), f32),
            jax.ShapeDtypeStruct((1, rank // n_row), f32),
            jax.ShapeDtypeStruct((tiles, strip), f32),
        ],
        in_specs=[SMEM] + [VMEM] * (4 + 2 * len(parts)),
        out_specs=[pl.BlockSpec(memory_space=pl.ANY), VMEM, VMEM],
        scratch_shapes=[
            pltpu.VMEM((tiles, strip, rank), bf16),
            pltpu.VMEM((tiles, strip, 2 * rank), f8),
            pltpu.VMEM((2, strip, rows // HALVES), f32),
            pltpu.SemaphoreType.DMA((2,)),
        ],
        compiler_params=pltpu.CompilerParams(vmem_limit_bytes=28 * MIB),
        cost_estimate=pl.CostEstimate(
            flops=4 * columns * rank * rows, bytes_accessed=4 * columns * rows, transcendentals=0
        ),
        name="update",
    )(where, sums, most, high, small, *parts, *cols)


def per_device(n_row, n_col, activations, out_grads, basis, row_moment, col_moment):
    chips = n_row // CORES
    columns, tokens = col_moment.shape[0], activations.shape[0] * n_col
    hidden = columns * n_col
    rank = basis.shape[1]
    width = -(-columns // (32 * chips)) * 32
    pad = width * chips - columns
    rows = width // CHUNKS
    ring = [0, 2, 4, 6, 7, 5, 3, 1] if n_col == 8 else list(range(n_col))
    hops = n_col // 2
    jobs, moves = [(0, 0, width, 0, 0)], [(0, 0, width)]
    for j in range(1, chips):
        for q in range(CHUNKS):
            at, part = q * rows, rows * (3 - q) // 5 // 128 * 128
            if j > 1 or part == 0:
                jobs.append((j, at, rows, len(moves), 0))
                moves.append((j, at, rows))
                continue
            jobs.append((j, at, part, len(moves), 0))
            if q == 0:
                jobs.append((j, at + part, rows - part, len(moves), part))
                moves.append((j, at, rows))
            else:
                jobs.append((j, at + part, rows - part, len(moves) + 1, 0))
                moves += [(j, at, part), (j, at + part, rows - part)]

    def to_sibling(value):
        return lax.ppermute(value, "row", [(r, r ^ 1) for r in range(n_row)])

    def to_chip(value, shift):
        pairs = [(r, (r + CORES * shift) % n_row) for r in range(n_row)]
        return lax.ppermute(value, "row", pairs)

    def around(value):
        pairs = [
            (r * n_col + ring[i], r * n_col + ring[(i + 1 - r % CORES * 2) % n_col])
            for r in range(n_row) for i in range(n_col)
        ]
        return lax.ppermute(value, ("row", "col"), pairs)

    def after(value, *others):
        return lax.optimization_barrier((value, others))[0]

    table = []
    for r in range(n_row):
        for c in range(n_col):
            p, x, k = ring.index(c), r // CORES, r % CORES
            entry = [k, int(c == 0), r, r ^ 1]
            for s in range(1, chips):
                there = (x - s) % chips
                entry += [CORES * there + k, CORES * there + 1 - k]
            way = 1 - 2 * k
            order = [p] + [p - way * s for s in range(1, hops + 1)]
            order += [p + way * s for s in range(1, hops + 1) if 2 * s != n_col]
            blocks_at = len(entry)
            entry += [ring[i % n_col] for i in order]
            starts_at = len(entry)
            entry += [((x + j) % chips * width + at) // 16 for j, at, *_ in jobs]
            sends_at = len(entry)
            entry += [
                ((x + s + j) % chips * width + at) // 16
                for j, at, _ in moves for s in range(1, chips)
            ]
            order_at = len(entry)
            entry += [(x + j) % chips * CHUNKS + q for j in range(chips) for q in range(CHUNKS)]
            table.append(entry)
    flat = lax.axis_index("row") * n_col + lax.axis_index("col")
    here = flat.astype(jnp.int32)[None]
    rows_at = 2

    mine, other = low_partial(here, activations, basis, n_col)
    table = np.array(table, np.int32)
    flat = after(flat.astype(jnp.uint32), other)
    where = lax.dynamic_slice(table, (flat, jnp.uint32(0)), (1, table.shape[1]))[0]
    mine = mine + to_sibling(other)
    arrived = [to_chip(mine, s) for s in range(1, chips)]

    grads = out_grads.T
    moment = after(col_moment, mine)[:, None]
    if pad:
        grads = jnp.pad(grads, ((0, pad), (0, 0)))
        moment = jnp.pad(moment, ((0, pad), (0, 0)), constant_values=1.0)
    grads = after(grads, other)
    sends = cut(where, grads, [size for _, _, size in moves for _ in range(1, chips)], sends_at)
    arrived = lax.optimization_barrier((*arrived, *sends))
    sends, arrived = arrived[chips - 1 :], arrived[: chips - 1]
    sends = [sends[n * (chips - 1) : (n + 1) * (chips - 1)] for n in range(len(moves))]
    mine = encode(mine, *arrived)
    moments = after(row_moment, mine)[None]
    moments = [moments, to_sibling(moments)]

    def exchange(send, *others):
        return [to_chip(after(value, *others), s) for s, value in enumerate(sends[send], 1)]

    def pass_on(got, *others):
        got = [after(value, *others) for value in got]
        return [both for value in got for both in (value, to_sibling(value))]

    got = {0: exchange(0, mine)}
    held = join(where, mine, to_sibling(mine))
    sibling = to_sibling(after(grads, held))
    blocks, siblings = [held], []
    for hop in range(1, hops + 1):
        moving = [around(held)]
        if hop > 1:
            moving.append(to_sibling(held))
        if hop == 2:
            turned = turn_basis(after(basis, held))
            moving += turned
        if hop == max(hops - 1, 1):
            moving += got[0]
        if hop == hops:
            known = [(block, n) for n, block in enumerate(blocks)]
            known += [(block, hops + 1 + n) for n, block in enumerate(siblings)]
            early = assemble(
                where, [block for block, _ in known], [blocks_at + n for _, n in known], tokens
            )
            moving += early
        moved = lax.optimization_barrier(tuple(moving))
        early = moved[-2:]
        held = moved[0]
        blocks.append(held)
        siblings += moved[1:2] if hop > 1 else []
        if hop == max(hops - 1, 1):
            passed = {0: pass_on(got[0], held)}
            for move in (1, 2):
                got[move] = exchange(move, held)
    if 2 * hops != n_col:
        siblings.append(to_sibling(held))
    known = len(known)
    late = [(held, hops)] + [
        (block, hops + 1 + n) for n, block in enumerate(siblings) if hops + n >= known
    ]
    high, low = assemble(
        where, [block for block, _ in late], [blocks_at + n for _, n in late], tokens, early
    )

    found = []

    def project_job(job, most):
        _, _, size, move, skip = jobs[job]
        part, col_next, sums, top = project(
            where, high, low, moment, most, [grads, sibling] + passed[move], skip,
            [] if job else moments, size, min(size, rows), starts_at + job, rows_at,
            0.0 if job else hidden * beta_two / (1.0 - beta_two),
        )
        found.append((part, col_next))
        return sums, top

    sums, top = project_job(0, jnp.zeros((1, rank), f32))
    sums = after(sums, *got[1], *got[2])
    passed[1] = pass_on(got[1], sums)
    hop, step = 0, 1
    while step < n_col:
        if hop == 0:
            arrived = [to_chip(sums, s) for s in range(1, chips)]
        else:
            arrived = [lax.ppermute(sums, "col", [(c, c ^ step) for c in range(n_col)])]
            step *= 2
        hop += 1
        if hop < len(jobs) and jobs[hop][3] in passed:
            _, top = project_job(hop, top)
            *arrived, top = lax.optimization_barrier((*arrived, top))
        sums = sum(arrived, sums)
        if hop == 1:
            passed[2] = pass_on(got[2], sums)
            for move in range(3, len(moves)):
                got[move] = exchange(move, sums)
        if hop == 3:
            for move in range(3, len(moves)):
                passed[move] = pass_on(got[move], sums)
    for job in range(len(found), len(jobs)):
        _, top = project_job(job, top)

    updated, row_next, col_next = update(
        where, sums, top, *turned, [part for part, _ in found], [col for _, col in found],
        rows, hidden, n_row, rows_at, order_at,
    )
    return (updated[:columns].T, row_next[0], col_next.reshape(-1)[:columns])


def solution(mesh):
    in_specs = (P("col", "row"), P("row", "col"), P("row", None), P("row"), P("col"))
    out_specs = (P("row", "col"), P("row"), P("col"))
    return jax.shard_map(
        functools.partial(per_device, mesh.shape["row"], mesh.shape["col"]),
        mesh=mesh, in_specs=in_specs, out_specs=out_specs, check_vma=False,
    )
```

```python
import functools

import jax
import jax.numpy as jnp
import numpy as np
from jax import lax
from jax.experimental import pallas as pl
from jax.experimental.pallas import tpu as pltpu
from jax.sharding import PartitionSpec as P

beta_two = 0.8
scale_alpha = 0.25
epsilon = 1e-30
CORES = 2
CHUNKS = 2
HALVES = 2
f32 = jnp.float32
bf16 = jnp.bfloat16
f8 = jnp.float8_e4m3fn
MIB = 1 << 20
CODE_TOP = 181.0
TOP_ROWS = 16
VMEM = pl.BlockSpec(memory_space=pltpu.VMEM)
SMEM = pl.BlockSpec(memory_space=pltpu.SMEM)


def split(value):
    high = value.astype(bf16)
    return high, (value - high.astype(f32)).astype(bf16)


def tile_of(size, most, unit):
    return max(t for t in range(unit, most + 1, unit) if size % t == 0)


def low_kernel(
    steps, n_col, here_ref, acts_ref, basis_ref, mine_ref, other_ref, act_ref, kept_ref, sem
):
    depth = basis_ref.shape[0]
    tile = depth // steps
    half = mine_ref.shape[1]
    copies, first = [], pltpu.make_async_copy(acts_ref, act_ref, sem.at[steps])
    first.start()
    for n in range(steps):
        at = pl.ds(n * tile, tile)
        copies.append(pltpu.make_async_copy(basis_ref.at[at, :], kept_ref.at[at, :], sem.at[n]))
    for copy in copies:
        copy.start()
    first.wait()
    total = None
    for n in range(steps):
        copies[n].wait()
        at = slice(n * tile, (n + 1) * tile)
        high, low = split(kept_ref[at, :])
        left = act_ref[:, at]
        one = jnp.dot(left, high, preferred_element_type=f32)
        one = one + jnp.dot(left, low, preferred_element_type=f32)
        total = one if total is None else total + one
    second = here_ref[0] // n_col % CORES == 1
    mine_ref[...] = jnp.where(second, total[:, half:], total[:, :half])
    other_ref[...] = jnp.where(second, total[:, :half], total[:, half:])


def low_partial(here, acts, basis, n_col):
    tokens, depth = acts.shape
    rank = basis.shape[1]
    steps = 8
    half = jax.ShapeDtypeStruct((tokens, rank // 2), f32)
    return pl.pallas_call(
        functools.partial(low_kernel, steps, n_col),
        out_shape=(half, half),
        in_specs=[SMEM] + [pl.BlockSpec(memory_space=pl.ANY)] * 2,
        out_specs=[VMEM] * 2,
        scratch_shapes=[
            pltpu.VMEM((tokens, depth), bf16),
            pltpu.VMEM((depth, rank), f32),
            pltpu.SemaphoreType.DMA((steps + 1,)),
        ],
        compiler_params=pltpu.CompilerParams(vmem_limit_bytes=60 * MIB),
        cost_estimate=pl.CostEstimate(
            flops=4 * tokens * depth * rank, bytes_accessed=6 * depth * rank, transcendentals=0
        ),
        name="low_partial",
    )(here, acts, basis)


def turn_kernel(basis_ref, high_ref, small_ref):
    rows, rank = basis_ref.shape
    tile = tile_of(rows, 256, 128)
    for begin in range(0, rows, tile):
        at = slice(begin, begin + tile)
        turned = basis_ref[at, :].T
        high = turned.astype(bf16)
        high_ref[:, at] = high
        small_ref[:rank, at] = ((turned - high.astype(f32)) * 2.0**20).astype(f8)
        small_ref[rank:, at] = (turned * 2.0**12).astype(f8)


def turn_basis(basis):
    rows, rank = basis.shape
    return pl.pallas_call(
        turn_kernel,
        out_shape=[
            jax.ShapeDtypeStruct((rank, rows), bf16),
            jax.ShapeDtypeStruct((2 * rank, rows), f8),
        ],
        in_specs=[VMEM],
        out_specs=[VMEM] * 2,
        compiler_params=pltpu.CompilerParams(vmem_limit_bytes=4 * MIB),
        cost_estimate=pl.CostEstimate(flops=0, bytes_accessed=8 * rows * rank, transcendentals=0),
        name="turn_basis",
    )(basis)


def add_kernel(first_ref, second_ref, out_ref):
    out_ref[...] = first_ref[...] + second_ref[...]


def add(first, second):
    return pl.pallas_call(
        add_kernel,
        out_shape=jax.ShapeDtypeStruct(first.shape, f32),
        in_specs=[VMEM] * 2,
        out_specs=VMEM,
        compiler_params=pltpu.CompilerParams(vmem_limit_bytes=4 * MIB),
        cost_estimate=pl.CostEstimate(flops=0, bytes_accessed=0, transcendentals=0),
        name="add",
    )(first, second)


def encode_kernel(*refs):
    out_ref = refs[-1]
    tokens, lanes = refs[0].shape
    value = refs[0][...]
    for ref in refs[1:-1]:
        value = value + ref[...]
    size = jnp.abs(value)
    top = (jnp.max(size, axis=0, keepdims=True) * (1.0 + 2.0**-7)).astype(bf16).astype(f32)
    top = jnp.maximum(top, 1e-36)
    code = size * (CODE_TOP / top)
    for _ in range(4):
        code = code * code
    out_ref[:tokens, :] = jnp.where(value < 0, -code, code).astype(bf16)
    out_ref[tokens:, :] = jnp.broadcast_to(top, (TOP_ROWS, lanes)).astype(bf16)


def encode(*blocks):
    tokens, lanes = blocks[0].shape
    return pl.pallas_call(
        encode_kernel,
        out_shape=jax.ShapeDtypeStruct((tokens + TOP_ROWS, lanes), bf16),
        in_specs=[VMEM] * len(blocks),
        out_specs=VMEM,
        compiler_params=pltpu.CompilerParams(vmem_limit_bytes=4 * MIB),
        cost_estimate=pl.CostEstimate(
            flops=0, bytes_accessed=8 * tokens * lanes, transcendentals=0
        ),
        name="encode",
    )(*blocks)


def decode(ref):
    tokens = ref.shape[0] - TOP_ROWS
    code = ref[:tokens, :].astype(f32)
    size = jnp.abs(code)
    for _ in range(4):
        size = lax.rsqrt(size)
    size = size * (ref[tokens : tokens + 1, :].astype(f32) * (1.0 / CODE_TOP))
    return jnp.where(code < 0, -size, size)


def join_kernel(where_ref, mine_ref, other_ref, out_ref):
    half = mine_ref.shape[1]
    core = where_ref[0]
    out_ref[:, pl.ds(pl.multiple_of(core * half, half), half)] = mine_ref[...]
    out_ref[:, pl.ds(pl.multiple_of((1 - core) * half, half), half)] = other_ref[...]


def join(where, mine, other):
    rows, half = mine.shape
    return pl.pallas_call(
        join_kernel,
        out_shape=jax.ShapeDtypeStruct((rows, 2 * half), bf16),
        in_specs=[SMEM, VMEM, VMEM],
        out_specs=VMEM,
        compiler_params=pltpu.CompilerParams(vmem_limit_bytes=4 * MIB),
        cost_estimate=pl.CostEstimate(flops=0, bytes_accessed=8 * rows * half, transcendentals=0),
        name="join",
    )(where, mine, other)


def assemble_kernel(blocks, offset, where_ref, *refs):
    high_ref, low_ref = refs[blocks:]
    for b, ref in enumerate(refs[:blocks]):
        tokens = ref.shape[0] - TOP_ROWS
        rows = pl.ds(pl.multiple_of(where_ref[offset + b] * tokens, tokens), tokens)
        high_ref[rows, :], low_ref[rows, :] = split(decode(ref))


def assemble(where, found, offset):
    blocks = len(found)
    rows, rank = found[0].shape
    shape = (blocks * (rows - TOP_ROWS), rank)
    return pl.pallas_call(
        functools.partial(assemble_kernel, blocks, offset),
        out_shape=[jax.ShapeDtypeStruct(shape, bf16)] * 2,
        in_specs=[SMEM] + [VMEM] * blocks,
        out_specs=[VMEM] * 2,
        compiler_params=pltpu.CompilerParams(vmem_limit_bytes=4 * MIB),
        cost_estimate=pl.CostEstimate(flops=0, bytes_accessed=0, transcendentals=0),
        name="assemble",
    )(where, *found)


def cut_kernel(starts_at, counts, where_ref, grads_ref, *refs):
    outs, sem = refs[:-1], refs[-1]
    copies = []
    for n, out in enumerate(outs):
        rows = out.shape[0]
        at = pl.ds(pl.multiple_of(where_ref[starts_at + n] * 16, 16), rows)
        copies.append(pltpu.make_async_copy(grads_ref.at[at, :], out, sem.at[n]))
    for copy in copies:
        copy.start()
    for copy in copies:
        copy.wait()


def cut(where, grads, sizes, starts_at):
    return pl.pallas_call(
        functools.partial(cut_kernel, starts_at, len(sizes)),
        out_shape=[jax.ShapeDtypeStruct((size, grads.shape[1]), bf16) for size in sizes],
        in_specs=[SMEM, pl.BlockSpec(memory_space=pl.ANY)],
        out_specs=[VMEM] * len(sizes),
        scratch_shapes=[pltpu.SemaphoreType.DMA((len(sizes),))],
        compiler_params=pltpu.CompilerParams(vmem_limit_bytes=4 * MIB),
        cost_estimate=pl.CostEstimate(
            flops=0, bytes_accessed=4 * sum(sizes) * grads.shape[1], transcendentals=0
        ),
        name="cut",
    )(where, grads)


def project_kernel(
    pieces, skip, step, start_at, rows_at, first, where_ref, high_ref, low_ref, moment_ref,
    most_ref, *refs
):
    out_ref, colnext_ref, sums_ref, top_ref = refs[len(refs) - 4 :]
    grads, moments = refs[:pieces], refs[pieces : len(refs) - 4]
    rows, rank = out_ref.shape
    tokens = grads[0].shape[1]
    order = [
        pl.ds(pl.multiple_of(where_ref[rows_at + p] * tokens, tokens), tokens)
        for p in range(pieces)
    ]
    high = jnp.concatenate([high_ref[at, :] for at in order], axis=0)
    low = jnp.concatenate([low_ref[at, :] for at in order], axis=0)
    sums = jnp.zeros((1, rank), f32)
    if first:
        lanes = moments[0].shape[1]
        owner = lax.broadcasted_iota(jnp.int32, (1, rank), 1) // lanes
        for n, ref in enumerate(moments):
            wide = jnp.concatenate([ref[...]] * (rank // lanes), axis=1)
            sums = jnp.where(owner == where_ref[rows_at + n], wide, sums)
        sums = sums * jnp.where(where_ref[1] == 1, first, 0.0)
    top = most_ref[...]
    for begin in range(0, rows, step):
        at = pl.ds(pl.multiple_of(where_ref[start_at] * 16 + begin, 16), step)
        here = slice(begin, begin + step)
        there = slice(skip + begin, skip + begin + step)
        grad = jnp.concatenate(
            [g[at, :] for g in grads[:2]] + [g[there, :] for g in grads[2:]], axis=1
        )
        total = jnp.dot(grad, high, preferred_element_type=f32) + jnp.dot(
            grad, low, preferred_element_type=f32
        )
        squares = total * total
        sums = sums + jnp.sum(squares, axis=0, keepdims=True)
        quarter = sum(squares[:, n : n + 128] for n in range(0, rank, 128))
        col_next = beta_two * moment_ref[at, :] + (1.0 - beta_two) * (
            jnp.sum(quarter, axis=1, keepdims=True) / rank + epsilon
        )
        part = total * lax.rsqrt(col_next)
        top = jnp.maximum(top, jnp.max(jnp.abs(part), axis=0, keepdims=True))
        out_ref[here, :] = part
        long = colnext_ref.shape[1]
        wide = jnp.broadcast_to(col_next, (step, 128))
        if long > step:
            wide = jnp.concatenate([wide, jnp.zeros((long - step, 128), f32)], axis=0)
        colnext_ref[begin // step : begin // step + 1, :] = wide.T[:1, :]
    sums_ref[...] = sums
    top_ref[...] = top


def project(
    where, high, low, moment, most, grads, skip, moments, rows, step, start_at, rows_at, first
):
    tokens, rank = high.shape
    long = -(-step // 128) * 128
    return pl.pallas_call(
        functools.partial(
            project_kernel, len(grads), skip, step, start_at, rows_at, first
        ),
        out_shape=[
            jax.ShapeDtypeStruct((rows, rank), f32),
            jax.ShapeDtypeStruct((rows // step, long), f32),
            jax.ShapeDtypeStruct((1, rank), f32),
            jax.ShapeDtypeStruct((1, rank), f32),
        ],
        in_specs=[SMEM] + [VMEM] * (4 + len(grads) + len(moments)),
        out_specs=[VMEM] * 4,
        compiler_params=pltpu.CompilerParams(vmem_limit_bytes=16 * MIB),
        cost_estimate=pl.CostEstimate(flops=0, bytes_accessed=0, transcendentals=0),
        name="project",
    )(where, high, low, moment, most, *grads, *moments)


def segments(refs, part_refs, tile):
    found, done = [], 0
    for ref, part_ref in zip(refs, part_refs):
        rows = part_ref.shape[0]
        for row in range(0, rows, tile):
            size = min(tile, rows - row)
            found.append((done // tile, done % tile, size, ref, row))
            done += size
    return found


def update_kernel(
    count, parts, rows_at, order_at, where_ref, sums_ref, most_ref, high_ref, small_ref, *refs
):
    part_refs, col_refs = refs[:parts], refs[parts : 2 * parts]
    out_ref, rownext_ref, colnext_ref, lhs_ref, lhs_small_ref, scale_ref = refs[2 * parts :]
    tiles, tile, rank = lhs_ref.shape
    step = pl.program_id(0)

    @pl.when(step == 0)
    def _():
        row_next = (1.0 - beta_two) * (sums_ref[...] / count + epsilon)
        rows = rownext_ref.shape[1]
        held = jnp.zeros((1, rows), f32)
        for r in range(rank // rows):
            held = jnp.where(where_ref[rows_at] == r, row_next[:, r * rows : (r + 1) * rows], held)
        rownext_ref[...] = held
        scale = scale_alpha * lax.rsqrt(row_next) * jnp.sqrt(
            jnp.mean(row_next, axis=1, keepdims=True)
        )
        strip = colnext_ref.shape[1]
        for n, begin, size, ref, row in segments(col_refs, part_refs, tile):
            strip = pl.ds(where_ref[order_at + n], 1)
            colnext_ref[strip, begin : begin + size] = ref[row // tile : row // tile + 1, :size]
        top = jnp.maximum(jnp.max(scale * most_ref[...], axis=1, keepdims=True), 1e-30)
        scale_ref[0:1, :] = scale
        scale_ref[1:2, :] = jnp.broadcast_to(2.0**7 / top, (1, rank))
        scale_ref[2:3, :] = jnp.broadcast_to(top * 2.0**-27, (1, rank))

    for number in range(tiles):

        @pl.when(step == number)
        def _():
            for n, begin, size, ref, row in segments(part_refs, part_refs, tile):
                if n != number:
                    continue
                value = ref[row : row + size, :] * scale_ref[0:1, :]
                high = value.astype(bf16)
                grow = scale_ref[1:2, :]
                at = slice(begin, begin + size)
                lhs_ref[number, at, :] = high
                lhs_small_ref[number, at, :rank] = (value * grow).astype(f8)
                lhs_small_ref[number, at, rank:] = (
                    (value - high.astype(f32)) * (grow * 2.0**8)
                ).astype(f8)

    now = step % tiles
    lanes = pl.ds(pl.multiple_of(step // tiles * out_ref.shape[1], 128), out_ref.shape[1])
    out_ref[...] = jnp.dot(
        lhs_ref[now], high_ref[:, lanes], preferred_element_type=f32
    ) + scale_ref[2:3, 0:1] * jnp.dot(
        lhs_small_ref[now], small_ref[:, lanes], preferred_element_type=f32
    )


def update(where, sums, most, high, small, parts, cols, strip, hidden, n_row, rows_at, order_at):
    rank, rows = high.shape
    columns = sum(part.shape[0] for part in parts)
    tiles = columns // strip
    wide = rows // HALVES
    return pl.pallas_call(
        functools.partial(update_kernel, float(hidden), len(parts), rows_at, order_at),
        out_shape=[
            jax.ShapeDtypeStruct((columns, rows), f32),
            jax.ShapeDtypeStruct((1, rank // n_row), f32),
            jax.ShapeDtypeStruct((tiles, strip), f32),
        ],
        grid_spec=pltpu.PrefetchScalarGridSpec(
            num_scalar_prefetch=1,
            grid=(tiles * HALVES,),
            in_specs=[VMEM] * (4 + 2 * len(parts)),
            out_specs=[
                pl.BlockSpec((strip, wide), lambda i, s: (s[order_at + i % tiles], i // tiles)),
                pl.BlockSpec((1, rank // n_row), lambda i, s: (0, 0)),
                pl.BlockSpec((tiles, strip), lambda i, s: (0, 0)),
            ],
            scratch_shapes=[
                pltpu.VMEM((tiles, strip, rank), bf16),
                pltpu.VMEM((tiles, strip, 2 * rank), f8),
                pltpu.VMEM((8, rank), f32),
            ],
        ),
        compiler_params=pltpu.CompilerParams(vmem_limit_bytes=28 * MIB),
        cost_estimate=pl.CostEstimate(
            flops=4 * columns * rank * rows, bytes_accessed=4 * columns * rows, transcendentals=0
        ),
        name="update",
    )(where, sums, most, high, small, *parts, *cols)


def per_device(n_row, n_col, activations, out_grads, basis, row_moment, col_moment):
    chips = n_row // CORES
    columns = col_moment.shape[0]
    hidden = columns * n_col
    rank = basis.shape[1]
    width = -(-columns // (32 * chips)) * 32
    pad = width * chips - columns
    rows = width // CHUNKS
    ring = [0, 2, 4, 6, 7, 5, 3, 1] if n_col == 8 else list(range(n_col))
    hops = n_col // 2
    jobs, moves = [(0, 0, width, 0, 0)], [(0, 0, width)]
    for j in range(1, chips):
        for q in range(CHUNKS):
            at, part = q * rows, rows * (3 - q) // 5 // 128 * 128
            if j > 1 or part == 0:
                jobs.append((j, at, rows, len(moves), 0))
                moves.append((j, at, rows))
                continue
            jobs.append((j, at, part, len(moves), 0))
            if q == 0:
                jobs.append((j, at + part, rows - part, len(moves), part))
                moves.append((j, at, rows))
            else:
                jobs.append((j, at + part, rows - part, len(moves) + 1, 0))
                moves += [(j, at, part), (j, at + part, rows - part)]

    def to_sibling(value):
        return lax.ppermute(value, "row", [(r, r ^ 1) for r in range(n_row)])

    def to_chip(value, shift):
        pairs = [(r, (r + CORES * shift) % n_row) for r in range(n_row)]
        return lax.ppermute(value, "row", pairs)

    def around(value):
        pairs = [
            (r * n_col + ring[i], r * n_col + ring[(i + 1 - r % CORES * 2) % n_col])
            for r in range(n_row) for i in range(n_col)
        ]
        return lax.ppermute(value, ("row", "col"), pairs)

    def after(value, *others):
        return lax.optimization_barrier((value, others))[0]

    table = []
    for r in range(n_row):
        for c in range(n_col):
            p, x, k = ring.index(c), r // CORES, r % CORES
            entry = [k, int(c == 0), r, r ^ 1]
            for s in range(1, chips):
                there = (x - s) % chips
                entry += [CORES * there + k, CORES * there + 1 - k]
            way = 1 - 2 * k
            order = [p] + [p - way * s for s in range(1, hops + 1)]
            order += [p + way * s for s in range(1, hops + 1) if 2 * s != n_col]
            blocks_at = len(entry)
            entry += [ring[i % n_col] for i in order]
            starts_at = len(entry)
            entry += [((x + j) % chips * width + at) // 16 for j, at, *_ in jobs]
            sends_at = len(entry)
            entry += [
                ((x + s + j) % chips * width + at) // 16
                for j, at, _ in moves for s in range(1, chips)
            ]
            order_at = len(entry)
            entry += [(x + j) % chips * CHUNKS + q for j in range(chips) for q in range(CHUNKS)]
            table.append(entry)
    flat = lax.axis_index("row") * n_col + lax.axis_index("col")
    here = flat.astype(jnp.int32)[None]
    rows_at = 2

    mine, other = low_partial(here, activations, basis, n_col)
    table = np.array(table, np.int32)
    flat = after(flat.astype(jnp.uint32), other)
    where = lax.dynamic_slice(table, (flat, jnp.uint32(0)), (1, table.shape[1]))[0]
    mine = add(mine, to_sibling(other))
    arrived = [to_chip(mine, s) for s in range(1, chips)]

    grads = out_grads.T
    moment = after(col_moment, mine)[:, None]
    if pad:
        grads = jnp.pad(grads, ((0, pad), (0, 0)))
        moment = jnp.pad(moment, ((0, pad), (0, 0)), constant_values=1.0)
    grads = after(grads, other)
    sends = cut(where, grads, [size for _, _, size in moves for _ in range(1, chips)], sends_at)
    arrived = lax.optimization_barrier((*arrived, *sends))
    sends, arrived = arrived[chips - 1 :], arrived[: chips - 1]
    sends = [sends[n * (chips - 1) : (n + 1) * (chips - 1)] for n in range(len(moves))]
    mine = encode(mine, *arrived)
    moments = after(row_moment, mine)[None]
    moments = [moments, to_sibling(moments)]

    def exchange(send, *others):
        return [to_chip(after(value, *others), s) for s, value in enumerate(sends[send], 1)]

    def pass_on(got, *others):
        got = [after(value, *others) for value in got]
        return [both for value in got for both in (value, to_sibling(value))]

    got = {0: exchange(0, mine)}
    held = join(where, mine, to_sibling(mine))
    sibling = to_sibling(after(grads, held))
    blocks, siblings = [held], []
    for hop in range(1, hops + 1):
        moving = [around(held)]
        if hop > 1:
            moving.append(to_sibling(held))
        if hop == 2:
            turned = turn_basis(after(basis, held))
            moving += turned
        if hop == max(hops - 1, 1):
            moving += got[0]
        moved = lax.optimization_barrier(tuple(moving))
        held = moved[0]
        blocks.append(held)
        siblings += moved[1:2] if hop > 1 else []
        if hop == max(hops - 1, 1):
            passed = {0: pass_on(got[0], held)}
            for move in (1, 2):
                got[move] = exchange(move, held)
    if 2 * hops != n_col:
        siblings.append(to_sibling(held))
    high, low = assemble(where, blocks + siblings, blocks_at)

    found = []

    def project_job(job, most):
        _, _, size, move, skip = jobs[job]
        part, col_next, sums, top = project(
            where, high, low, moment, most, [grads, sibling] + passed[move], skip,
            [] if job else moments, size, min(size, rows), starts_at + job, rows_at,
            0.0 if job else hidden * beta_two / (1.0 - beta_two),
        )
        found.append((part, col_next))
        return sums, top

    sums, top = project_job(0, jnp.zeros((1, rank), f32))
    sums = after(sums, *got[1], *got[2])
    passed[1] = pass_on(got[1], sums)
    hop, step = 0, 1
    while step < n_col:
        if hop == 0:
            arrived = [to_chip(sums, s) for s in range(1, chips)]
        else:
            arrived = [lax.ppermute(sums, "col", [(c, c ^ step) for c in range(n_col)])]
            step *= 2
        hop += 1
        if hop < len(jobs) and jobs[hop][3] in passed:
            _, top = project_job(hop, top)
            *arrived, top = lax.optimization_barrier((*arrived, top))
        sums = sum(arrived, sums)
        if hop == 1:
            passed[2] = pass_on(got[2], sums)
            for move in range(3, len(moves)):
                got[move] = exchange(move, sums)
        if hop == 3:
            for move in range(3, len(moves)):
                passed[move] = pass_on(got[move], sums)
    for job in range(len(found), len(jobs)):
        _, top = project_job(job, top)

    updated, row_next, col_next = update(
        where, sums, top, *turned, [part for part, _ in found], [col for _, col in found],
        rows, hidden, n_row, rows_at, order_at,
    )
    return (updated[:columns].T, row_next[0], col_next.reshape(-1)[:columns])


def solution(mesh):
    in_specs = (P("col", "row"), P("row", "col"), P("row", None), P("row"), P("col"))
    out_specs = (P("row", "col"), P("row"), P("col"))
    return jax.shard_map(
        functools.partial(per_device, mesh.shape["row"], mesh.shape["col"]),
        mesh=mesh, in_specs=in_specs, out_specs=out_specs, check_vma=False,
    )
```

```python
import functools

import jax
import jax.numpy as jnp
import numpy as np
from jax import lax
from jax.experimental import pallas as pl
from jax.experimental.pallas import tpu as pltpu
from jax.sharding import PartitionSpec as P

beta_two = 0.8
scale_alpha = 0.25
epsilon = 1e-30
CORES = 2
CHUNKS = 2
HALVES = 2
f32 = jnp.float32
bf16 = jnp.bfloat16
f8 = jnp.float8_e4m3fn
MIB = 1 << 20
CODE_TOP = 181.0
TOP_ROWS = 16
VMEM = pl.BlockSpec(memory_space=pltpu.VMEM)
SMEM = pl.BlockSpec(memory_space=pltpu.SMEM)


def split(value):
    high = value.astype(bf16)
    return high, (value - high.astype(f32)).astype(bf16)


def tile_of(size, most, unit):
    return max(t for t in range(unit, most + 1, unit) if size % t == 0)


def low_kernel(
    steps, n_col, here_ref, acts_ref, basis_ref, mine_ref, other_ref, act_ref, kept_ref, sem
):
    depth = basis_ref.shape[0]
    tile = depth // steps
    half = mine_ref.shape[1]
    copies, first = [], pltpu.make_async_copy(acts_ref, act_ref, sem.at[steps])
    first.start()
    for n in range(steps):
        at = pl.ds(n * tile, tile)
        copies.append(pltpu.make_async_copy(basis_ref.at[at, :], kept_ref.at[at, :], sem.at[n]))
    for copy in copies:
        copy.start()
    first.wait()
    total = None
    for n in range(steps):
        copies[n].wait()
        at = slice(n * tile, (n + 1) * tile)
        high, low = split(kept_ref[at, :])
        left = act_ref[:, at]
        one = jnp.dot(left, high, preferred_element_type=f32)
        one = one + jnp.dot(left, low, preferred_element_type=f32)
        total = one if total is None else total + one
    second = here_ref[0] // n_col % CORES == 1
    mine_ref[...] = jnp.where(second, total[:, half:], total[:, :half])
    other_ref[...] = jnp.where(second, total[:, :half], total[:, half:])


def low_partial(here, acts, basis, n_col):
    tokens, depth = acts.shape
    rank = basis.shape[1]
    steps = 8
    half = jax.ShapeDtypeStruct((tokens, rank // 2), f32)
    return pl.pallas_call(
        functools.partial(low_kernel, steps, n_col),
        out_shape=(half, half),
        in_specs=[SMEM] + [pl.BlockSpec(memory_space=pl.ANY)] * 2,
        out_specs=[VMEM] * 2,
        scratch_shapes=[
            pltpu.VMEM((tokens, depth), bf16),
            pltpu.VMEM((depth, rank), f32),
            pltpu.SemaphoreType.DMA((steps + 1,)),
        ],
        compiler_params=pltpu.CompilerParams(vmem_limit_bytes=60 * MIB),
        cost_estimate=pl.CostEstimate(
            flops=4 * tokens * depth * rank, bytes_accessed=6 * depth * rank, transcendentals=0
        ),
        name="low_partial",
    )(here, acts, basis)


def turn_kernel(basis_ref, high_ref, small_ref):
    rows, rank = basis_ref.shape
    tile = tile_of(rows, 256, 128)
    for begin in range(0, rows, tile):
        at = slice(begin, begin + tile)
        turned = basis_ref[at, :].T
        high = turned.astype(bf16)
        high_ref[:, at] = high
        small_ref[:rank, at] = ((turned - high.astype(f32)) * 2.0**20).astype(f8)
        small_ref[rank:, at] = (turned * 2.0**12).astype(f8)


def turn_basis(basis):
    rows, rank = basis.shape
    return pl.pallas_call(
        turn_kernel,
        out_shape=[
            jax.ShapeDtypeStruct((rank, rows), bf16),
            jax.ShapeDtypeStruct((2 * rank, rows), f8),
        ],
        in_specs=[VMEM],
        out_specs=[VMEM] * 2,
        compiler_params=pltpu.CompilerParams(vmem_limit_bytes=4 * MIB),
        cost_estimate=pl.CostEstimate(flops=0, bytes_accessed=8 * rows * rank, transcendentals=0),
        name="turn_basis",
    )(basis)


def add_kernel(first_ref, second_ref, out_ref):
    out_ref[...] = first_ref[...] + second_ref[...]


def add(first, second):
    return pl.pallas_call(
        add_kernel,
        out_shape=jax.ShapeDtypeStruct(first.shape, f32),
        in_specs=[VMEM] * 2,
        out_specs=VMEM,
        compiler_params=pltpu.CompilerParams(vmem_limit_bytes=4 * MIB),
        cost_estimate=pl.CostEstimate(flops=0, bytes_accessed=0, transcendentals=0),
        name="add",
    )(first, second)


def encode_kernel(*refs):
    out_ref = refs[-1]
    tokens, lanes = refs[0].shape
    value = refs[0][...]
    for ref in refs[1:-1]:
        value = value + ref[...]
    size = jnp.abs(value)
    top = (jnp.max(size, axis=0, keepdims=True) * (1.0 + 2.0**-7)).astype(bf16).astype(f32)
    top = jnp.maximum(top, 1e-36)
    code = size * (CODE_TOP / top)
    for _ in range(4):
        code = code * code
    out_ref[:tokens, :] = jnp.where(value < 0, -code, code).astype(bf16)
    out_ref[tokens:, :] = jnp.broadcast_to(top, (TOP_ROWS, lanes)).astype(bf16)


def encode(*blocks):
    tokens, lanes = blocks[0].shape
    return pl.pallas_call(
        encode_kernel,
        out_shape=jax.ShapeDtypeStruct((tokens + TOP_ROWS, lanes), bf16),
        in_specs=[VMEM] * len(blocks),
        out_specs=VMEM,
        compiler_params=pltpu.CompilerParams(vmem_limit_bytes=4 * MIB),
        cost_estimate=pl.CostEstimate(
            flops=0, bytes_accessed=8 * tokens * lanes, transcendentals=0
        ),
        name="encode",
    )(*blocks)


def decode(ref):
    tokens = ref.shape[0] - TOP_ROWS
    code = ref[:tokens, :].astype(f32)
    size = jnp.abs(code)
    for _ in range(4):
        size = lax.rsqrt(size)
    size = size * (ref[tokens : tokens + 1, :].astype(f32) * (1.0 / CODE_TOP))
    return jnp.where(code < 0, -size, size)


def join_kernel(where_ref, mine_ref, other_ref, out_ref):
    half = mine_ref.shape[1]
    core = where_ref[0]
    out_ref[:, pl.ds(pl.multiple_of(core * half, half), half)] = mine_ref[...]
    out_ref[:, pl.ds(pl.multiple_of((1 - core) * half, half), half)] = other_ref[...]


def join(where, mine, other):
    rows, half = mine.shape
    return pl.pallas_call(
        join_kernel,
        out_shape=jax.ShapeDtypeStruct((rows, 2 * half), bf16),
        in_specs=[SMEM, VMEM, VMEM],
        out_specs=VMEM,
        compiler_params=pltpu.CompilerParams(vmem_limit_bytes=4 * MIB),
        cost_estimate=pl.CostEstimate(flops=0, bytes_accessed=8 * rows * half, transcendentals=0),
        name="join",
    )(where, mine, other)


def assemble_kernel(blocks, offset, where_ref, *refs):
    high_ref, low_ref = refs[blocks:]
    for b, ref in enumerate(refs[:blocks]):
        tokens = ref.shape[0] - TOP_ROWS
        rows = pl.ds(pl.multiple_of(where_ref[offset + b] * tokens, tokens), tokens)
        high_ref[rows, :], low_ref[rows, :] = split(decode(ref))


def assemble(where, found, offset):
    blocks = len(found)
    rows, rank = found[0].shape
    shape = (blocks * (rows - TOP_ROWS), rank)
    return pl.pallas_call(
        functools.partial(assemble_kernel, blocks, offset),
        out_shape=[jax.ShapeDtypeStruct(shape, bf16)] * 2,
        in_specs=[SMEM] + [VMEM] * blocks,
        out_specs=[VMEM] * 2,
        compiler_params=pltpu.CompilerParams(vmem_limit_bytes=4 * MIB),
        cost_estimate=pl.CostEstimate(flops=0, bytes_accessed=0, transcendentals=0),
        name="assemble",
    )(where, *found)


def cut_kernel(starts_at, counts, where_ref, grads_ref, *refs):
    outs, sem = refs[:-1], refs[-1]
    copies = []
    for n, out in enumerate(outs):
        rows = out.shape[0]
        at = pl.ds(pl.multiple_of(where_ref[starts_at + n] * 16, 16), rows)
        copies.append(pltpu.make_async_copy(grads_ref.at[at, :], out, sem.at[n]))
    for copy in copies:
        copy.start()
    for copy in copies:
        copy.wait()


def cut(where, grads, sizes, starts_at):
    return pl.pallas_call(
        functools.partial(cut_kernel, starts_at, len(sizes)),
        out_shape=[jax.ShapeDtypeStruct((size, grads.shape[1]), bf16) for size in sizes],
        in_specs=[SMEM, pl.BlockSpec(memory_space=pl.ANY)],
        out_specs=[VMEM] * len(sizes),
        scratch_shapes=[pltpu.SemaphoreType.DMA((len(sizes),))],
        compiler_params=pltpu.CompilerParams(vmem_limit_bytes=4 * MIB),
        cost_estimate=pl.CostEstimate(
            flops=0, bytes_accessed=4 * sum(sizes) * grads.shape[1], transcendentals=0
        ),
        name="cut",
    )(where, grads)


def project_kernel(
    pieces, skip, step, start_at, rows_at, first, where_ref, high_ref, low_ref, moment_ref,
    most_ref, *refs
):
    out_ref, colnext_ref, sums_ref, top_ref = refs[len(refs) - 4 :]
    grads, moments = refs[:pieces], refs[pieces : len(refs) - 4]
    rows, rank = out_ref.shape
    sums = jnp.zeros((1, rank), f32)
    if first:
        lanes = moments[0].shape[1]
        owner = lax.broadcasted_iota(jnp.int32, (1, rank), 1) // lanes
        for n, ref in enumerate(moments):
            wide = jnp.concatenate([ref[...]] * (rank // lanes), axis=1)
            sums = jnp.where(owner == where_ref[rows_at + n], wide, sums)
        sums = sums * jnp.where(where_ref[1] == 1, first, 0.0)
    top = most_ref[...]
    for begin in range(0, rows, step):
        at = pl.ds(pl.multiple_of(where_ref[start_at] * 16 + begin, 16), step)
        here = slice(begin, begin + step)
        there = slice(skip + begin, skip + begin + step)
        grad = jnp.concatenate(
            [g[at, :] for g in grads[:2]] + [g[there, :] for g in grads[2:]], axis=1
        )
        total = jnp.dot(grad, high_ref[...], preferred_element_type=f32) + jnp.dot(
            grad, low_ref[...], preferred_element_type=f32
        )
        squares = total * total
        sums = sums + jnp.sum(squares, axis=0, keepdims=True)
        quarter = sum(squares[:, n : n + 128] for n in range(0, rank, 128))
        col_next = beta_two * moment_ref[at, :] + (1.0 - beta_two) * (
            jnp.sum(quarter, axis=1, keepdims=True) / rank + epsilon
        )
        part = total * lax.rsqrt(col_next)
        top = jnp.maximum(top, jnp.max(jnp.abs(part), axis=0, keepdims=True))
        out_ref[here, :] = part
        long = colnext_ref.shape[1]
        wide = jnp.broadcast_to(col_next, (step, 128))
        if long > step:
            wide = jnp.concatenate([wide, jnp.zeros((long - step, 128), f32)], axis=0)
        colnext_ref[begin // step : begin // step + 1, :] = wide.T[:1, :]
    sums_ref[...] = sums
    top_ref[...] = top


def project(
    where, high, low, moment, most, grads, skip, moments, rows, step, start_at, rows_at, first
):
    tokens, rank = high.shape
    long = -(-step // 128) * 128
    return pl.pallas_call(
        functools.partial(
            project_kernel, len(grads), skip, step, start_at, rows_at, first
        ),
        out_shape=[
            jax.ShapeDtypeStruct((rows, rank), f32),
            jax.ShapeDtypeStruct((rows // step, long), f32),
            jax.ShapeDtypeStruct((1, rank), f32),
            jax.ShapeDtypeStruct((1, rank), f32),
        ],
        in_specs=[SMEM] + [VMEM] * (4 + len(grads) + len(moments)),
        out_specs=[VMEM] * 4,
        compiler_params=pltpu.CompilerParams(vmem_limit_bytes=16 * MIB),
        cost_estimate=pl.CostEstimate(flops=0, bytes_accessed=0, transcendentals=0),
        name="project",
    )(where, high, low, moment, most, *grads, *moments)


def segments(refs, part_refs, tile):
    found, done = [], 0
    for ref, part_ref in zip(refs, part_refs):
        rows = part_ref.shape[0]
        for row in range(0, rows, tile):
            size = min(tile, rows - row)
            found.append((done // tile, done % tile, size, ref, row))
            done += size
    return found


def update_kernel(
    count, parts, rows_at, order_at, where_ref, sums_ref, most_ref, high_ref, small_ref, *refs
):
    part_refs, col_refs = refs[:parts], refs[parts : 2 * parts]
    out_ref, rownext_ref, colnext_ref, lhs_ref, lhs_small_ref, scale_ref = refs[2 * parts :]
    tiles, tile, rank = lhs_ref.shape
    step = pl.program_id(0)

    @pl.when(step == 0)
    def _():
        row_next = (1.0 - beta_two) * (sums_ref[...] / count + epsilon)
        rows = rownext_ref.shape[1]
        held = jnp.zeros((1, rows), f32)
        for r in range(rank // rows):
            held = jnp.where(where_ref[rows_at] == r, row_next[:, r * rows : (r + 1) * rows], held)
        rownext_ref[...] = held
        scale = scale_alpha * lax.rsqrt(row_next) * jnp.sqrt(
            jnp.mean(row_next, axis=1, keepdims=True)
        )
        strip = colnext_ref.shape[1]
        for n, begin, size, ref, row in segments(col_refs, part_refs, tile):
            strip = pl.ds(where_ref[order_at + n], 1)
            colnext_ref[strip, begin : begin + size] = ref[row // tile : row // tile + 1, :size]
        top = jnp.maximum(jnp.max(scale * most_ref[...], axis=1, keepdims=True), 1e-30)
        scale_ref[0:1, :] = scale
        scale_ref[1:2, :] = jnp.broadcast_to(2.0**7 / top, (1, rank))
        scale_ref[2:3, :] = jnp.broadcast_to(top * 2.0**-27, (1, rank))

    for number in range(tiles):

        @pl.when(step == number)
        def _():
            for n, begin, size, ref, row in segments(part_refs, part_refs, tile):
                if n != number:
                    continue
                value = ref[row : row + size, :] * scale_ref[0:1, :]
                high = value.astype(bf16)
                grow = scale_ref[1:2, :]
                at = slice(begin, begin + size)
                lhs_ref[number, at, :] = high
                lhs_small_ref[number, at, :rank] = (value * grow).astype(f8)
                lhs_small_ref[number, at, rank:] = (
                    (value - high.astype(f32)) * (grow * 2.0**8)
                ).astype(f8)

    now = step % tiles
    lanes = pl.ds(pl.multiple_of(step // tiles * out_ref.shape[1], 128), out_ref.shape[1])
    out_ref[...] = jnp.dot(
        lhs_ref[now], high_ref[:, lanes], preferred_element_type=f32
    ) + scale_ref[2:3, 0:1] * jnp.dot(
        lhs_small_ref[now], small_ref[:, lanes], preferred_element_type=f32
    )


def update(where, sums, most, high, small, parts, cols, strip, hidden, n_row, rows_at, order_at):
    rank, rows = high.shape
    columns = sum(part.shape[0] for part in parts)
    tiles = columns // strip
    wide = rows // HALVES
    return pl.pallas_call(
        functools.partial(update_kernel, float(hidden), len(parts), rows_at, order_at),
        out_shape=[
            jax.ShapeDtypeStruct((columns, rows), f32),
            jax.ShapeDtypeStruct((1, rank // n_row), f32),
            jax.ShapeDtypeStruct((tiles, strip), f32),
        ],
        grid_spec=pltpu.PrefetchScalarGridSpec(
            num_scalar_prefetch=1,
            grid=(tiles * HALVES,),
            in_specs=[VMEM] * (4 + 2 * len(parts)),
            out_specs=[
                pl.BlockSpec((strip, wide), lambda i, s: (s[order_at + i % tiles], i // tiles)),
                pl.BlockSpec((1, rank // n_row), lambda i, s: (0, 0)),
                pl.BlockSpec((tiles, strip), lambda i, s: (0, 0)),
            ],
            scratch_shapes=[
                pltpu.VMEM((tiles, strip, rank), bf16),
                pltpu.VMEM((tiles, strip, 2 * rank), f8),
                pltpu.VMEM((8, rank), f32),
            ],
        ),
        compiler_params=pltpu.CompilerParams(vmem_limit_bytes=28 * MIB),
        cost_estimate=pl.CostEstimate(
            flops=4 * columns * rank * rows, bytes_accessed=4 * columns * rows, transcendentals=0
        ),
        name="update",
    )(where, sums, most, high, small, *parts, *cols)


def per_device(n_row, n_col, activations, out_grads, basis, row_moment, col_moment):
    chips = n_row // CORES
    columns = col_moment.shape[0]
    hidden = columns * n_col
    rank = basis.shape[1]
    width = -(-columns // (32 * chips)) * 32
    pad = width * chips - columns
    rows = width // CHUNKS
    ring = [0, 2, 4, 6, 7, 5, 3, 1] if n_col == 8 else list(range(n_col))
    hops = n_col // 2
    jobs, moves = [(0, 0, width, 0, 0)], [(0, 0, width)]
    for j in range(1, chips):
        for q in range(CHUNKS):
            at, part = q * rows, rows * (3 - q) // 5 // 128 * 128
            if j > 1 or part == 0:
                jobs.append((j, at, rows, len(moves), 0))
                moves.append((j, at, rows))
                continue
            jobs.append((j, at, part, len(moves), 0))
            if q == 0:
                jobs.append((j, at + part, rows - part, len(moves), part))
                moves.append((j, at, rows))
            else:
                jobs.append((j, at + part, rows - part, len(moves) + 1, 0))
                moves += [(j, at, part), (j, at + part, rows - part)]

    def to_sibling(value):
        return lax.ppermute(value, "row", [(r, r ^ 1) for r in range(n_row)])

    def to_chip(value, shift):
        pairs = [(r, (r + CORES * shift) % n_row) for r in range(n_row)]
        return lax.ppermute(value, "row", pairs)

    def around(value):
        pairs = [
            (r * n_col + ring[i], r * n_col + ring[(i + 1 - r % CORES * 2) % n_col])
            for r in range(n_row) for i in range(n_col)
        ]
        return lax.ppermute(value, ("row", "col"), pairs)

    def after(value, *others):
        return lax.optimization_barrier((value, others))[0]

    table = []
    for r in range(n_row):
        for c in range(n_col):
            p, x, k = ring.index(c), r // CORES, r % CORES
            entry = [k, int(c == 0), r, r ^ 1]
            for s in range(1, chips):
                there = (x - s) % chips
                entry += [CORES * there + k, CORES * there + 1 - k]
            way = 1 - 2 * k
            order = [p] + [p - way * s for s in range(1, hops + 1)]
            order += [p + way * s for s in range(1, hops + 1) if 2 * s != n_col]
            blocks_at = len(entry)
            each = n_col // n_row
            sources = entry[2:]
            order = [ring[i % n_col] for i in order]
            entry += [sources.index(block // each) * each + block % each for block in order]
            starts_at = len(entry)
            entry += [((x + j) % chips * width + at) // 16 for j, at, *_ in jobs]
            sends_at = len(entry)
            entry += [
                ((x + s + j) % chips * width + at) // 16
                for j, at, _ in moves for s in range(1, chips)
            ]
            order_at = len(entry)
            entry += [(x + j) % chips * CHUNKS + q for j in range(chips) for q in range(CHUNKS)]
            table.append(entry)
    flat = lax.axis_index("row") * n_col + lax.axis_index("col")
    here = flat.astype(jnp.int32)[None]
    rows_at = 2

    mine, other = low_partial(here, activations, basis, n_col)
    table = np.array(table, np.int32)
    flat = after(flat.astype(jnp.uint32), other)
    where = lax.dynamic_slice(table, (flat, jnp.uint32(0)), (1, table.shape[1]))[0]
    mine = add(mine, to_sibling(other))
    arrived = [to_chip(mine, s) for s in range(1, chips)]

    grads = out_grads.T
    moment = after(col_moment, mine)[:, None]
    if pad:
        grads = jnp.pad(grads, ((0, pad), (0, 0)))
        moment = jnp.pad(moment, ((0, pad), (0, 0)), constant_values=1.0)
    grads = after(grads, other)
    sends = cut(where, grads, [size for _, _, size in moves for _ in range(1, chips)], sends_at)
    arrived = lax.optimization_barrier((*arrived, *sends))
    sends, arrived = arrived[chips - 1 :], arrived[: chips - 1]
    sends = [sends[n * (chips - 1) : (n + 1) * (chips - 1)] for n in range(len(moves))]
    mine = encode(mine, *arrived)
    moments = after(row_moment, mine)[None]
    moments = [moments, to_sibling(moments)]

    def exchange(send, *others):
        return [to_chip(after(value, *others), s) for s, value in enumerate(sends[send], 1)]

    def pass_on(got, *others):
        got = [after(value, *others) for value in got]
        return [both for value in got for both in (value, to_sibling(value))]

    got = {0: exchange(0, mine)}
    held = join(where, mine, to_sibling(mine))
    sibling = to_sibling(after(grads, held))
    blocks, siblings = [held], []
    for hop in range(1, hops + 1):
        moving = [around(held)]
        if hop > 1:
            moving.append(to_sibling(held))
        if hop == 2:
            turned = turn_basis(after(basis, held))
            moving += turned
        if hop == max(hops - 1, 1):
            moving += got[0]
        moved = lax.optimization_barrier(tuple(moving))
        held = moved[0]
        blocks.append(held)
        siblings += moved[1:2] if hop > 1 else []
        if hop == max(hops - 1, 1):
            passed = {0: pass_on(got[0], held)}
            for move in (1, 2):
                got[move] = exchange(move, held)
    if 2 * hops != n_col:
        siblings.append(to_sibling(held))
    high, low = assemble(where, blocks + siblings, blocks_at)

    found = []

    def project_job(job, most):
        _, _, size, move, skip = jobs[job]
        part, col_next, sums, top = project(
            where, high, low, moment, most, [grads, sibling] + passed[move], skip,
            [] if job else moments, size, min(size, rows), starts_at + job, rows_at,
            0.0 if job else hidden * beta_two / (1.0 - beta_two),
        )
        found.append((part, col_next))
        return sums, top

    sums, top = project_job(0, jnp.zeros((1, rank), f32))
    sums = after(sums, *got[1], *got[2])
    passed[1] = pass_on(got[1], sums)
    hop, step = 0, 1
    while step < n_col:
        if hop == 0:
            arrived = [to_chip(sums, s) for s in range(1, chips)]
        else:
            arrived = [lax.ppermute(sums, "col", [(c, c ^ step) for c in range(n_col)])]
            step *= 2
        hop += 1
        if hop < len(jobs) and jobs[hop][3] in passed:
            _, top = project_job(hop, top)
            *arrived, top = lax.optimization_barrier((*arrived, top))
        sums = sum(arrived, sums)
        if hop == 1:
            passed[2] = pass_on(got[2], sums)
            for move in range(3, len(moves)):
                got[move] = exchange(move, sums)
        if hop == 3:
            for move in range(3, len(moves)):
                passed[move] = pass_on(got[move], sums)
    for job in range(len(found), len(jobs)):
        _, top = project_job(job, top)

    updated, row_next, col_next = update(
        where, sums, top, *turned, [part for part, _ in found], [col for _, col in found],
        rows, hidden, n_row, rows_at, order_at,
    )
    return (updated[:columns].T, row_next[0], col_next.reshape(-1)[:columns])


def solution(mesh):
    in_specs = (P("col", "row"), P("row", "col"), P("row", None), P("row"), P("col"))
    out_specs = (P("row", "col"), P("row"), P("col"))
    return jax.shard_map(
        functools.partial(per_device, mesh.shape["row"], mesh.shape["col"]),
        mesh=mesh, in_specs=in_specs, out_specs=out_specs, check_vma=False,
    )
```
